768 devices in a mesh: circ: 16 (over y_lo, x), axial: 24 (over z, y_hi), rad: 2 (over core).
Axes of the slice: x: 4, y: 8 (y_hi: 2, y_lo: 4; y = y_hi * 4 + y_lo), z: 12, core: 2. Of those that a mesh axis runs over, the one named last changes fastest.
Arguments:
- flow: float32 [6, 64, 192, 256], P(None, 'circ', 'axial', 'rad'), may hold values from -0.3 to 1.2, as said below
- inflow: float32 [6, 64, 256], replicated, may hold values from -0.3 to 1.2, as said below
- wall_kind: int32 [192, 2], replicated, may hold values from 0 to 1
Outputs:
- advanced: float32 [6, 64, 192, 256], P(None, 'circ', 'axial', 'rad')
The draws below stay inside these ranges and needn't reach their ends.
Inputs may be any that keep to these rules, and one draw needn't show every extreme that they name: `flow`: density and pressure lie in 0.8 to 1.2, circumferential velocity in -0.3 to 0.3, axial velocity in 0.2 to 0.6, radial velocity in -0.2 to 0.2, turbulence variable in 0.2 to 1.0. `inflow`: components lie in the same ranges as those of flow.
All inputs are finite; a program needn't handle non-finite values.
Results may differ from the reference program's by a relative error of at most 0.0003.
Values sent between devices are 32-bit elements; how exact they have to be, the bound alone decides.
A program may use at most 32 MiB of HBM per device.

```python
from functools import reduce
import jax
import jax.numpy as jnp
from jax import lax

NC = 64
NA = 192
NR = 256


def state_law(key, shape):
    lower = jnp.array([0.8, -0.3, 0.2, -0.2, 0.8, 0.2], jnp.float32)
    upper = jnp.array([1.2, 0.3, 0.6, 0.2, 1.2, 1.0], jnp.float32)
    unit = jax.random.uniform(key, shape, jnp.float32)
    lower = lower.reshape((6,) + (1,) * (len(shape) - 1))
    upper = upper.reshape((6,) + (1,) * (len(shape) - 1))
    return lower + (upper - lower) * unit


def draw_flow(key, part):
    key = jax.random.fold_in(key, 1)
    return state_law(key, (6, NC, NA, NR))


def draw_inflow(key, part):
    key = jax.random.fold_in(key, 2)
    return state_law(key, (6, NC, NR))


def touch_ends(entries, rng, low, top_value):
    place = [jax.random.randint(jax.random.fold_in(rng, axis), (), 0, length) for axis, length in enumerate(entries.shape)]
    longest = entries.shape.index(max(entries.shape))
    next_to = place[:longest] + [(place[longest] + 1) % entries.shape[longest]] + place[longest + 1:]
    return entries.at[tuple(place)].set(low).at[tuple(next_to)].set(top_value)


def setup_inputs(seed: int = 0) -> dict:
    keys = jax.random.split(jax.random.key(seed), 4)
    flow = draw_flow(jax.random.fold_in(keys[3], 71), 0)
    inflow = draw_inflow(jax.random.fold_in(keys[3], 71), 0)
    wall_kind = touch_ends(jax.random.randint(keys[2], (NA, 2), 0, 2), jax.random.fold_in(keys[2], 1), 0, 1).astype(jnp.int32)
    return dict(flow=flow, inflow=inflow, wall_kind=wall_kind)


GAMMA = 1.4
STEP_SIZE = 0.15
LIMIT_EPS = 0.03
FIX_WIDTH = 0.2
PRODUCE = 0.1355
DESTROY = 3.24

def conserved(prim):
    density = prim[0]
    energy = prim[4] / (GAMMA - 1.0) + 0.5 * density * (prim[1] * prim[1] + prim[2] * prim[2] + prim[3] * prim[3])
    return jnp.stack([density, density * prim[1], density * prim[2], density * prim[3], energy, density * prim[5]])

def primitive(cons):
    density = cons[0]
    vel_c = cons[1] / density
    vel_a = cons[2] / density
    vel_r = cons[3] / density
    pressure = (GAMMA - 1.0) * (cons[4] - 0.5 * density * (vel_c * vel_c + vel_a * vel_a + vel_r * vel_r))
    return jnp.stack([density, vel_c, vel_a, vel_r, pressure, cons[5] / density])

def reflect(cells, kinds):
    noslip = jnp.where(kinds == 1, -1.0, 1.0)[None, :, None]
    return jnp.stack([cells[0], noslip * cells[1], noslip * cells[2], -cells[3], cells[4], noslip * cells[5]])

def venkat(upper, lower, delta):
    bound = jnp.where(delta > 0.0, upper, lower)
    top = bound * bound + LIMIT_EPS + 2.0 * delta * bound
    bottom = bound * bound + 2.0 * delta * delta + bound * delta + LIMIT_EPS
    return top / bottom

def limited(extended):
    centre = extended[:, 1:-1, 1:-1, 1:-1]
    beside_all = [extended[:, 2:, 1:-1, 1:-1], extended[:, :-2, 1:-1, 1:-1], extended[:, 1:-1, 2:, 1:-1], extended[:, 1:-1, :-2, 1:-1], extended[:, 1:-1, 1:-1, 2:], extended[:, 1:-1, 1:-1, :-2]]
    grads = [0.5 * (beside_all[0] - beside_all[1]), 0.5 * (beside_all[2] - beside_all[3]), 0.5 * (beside_all[4] - beside_all[5])]
    upper = reduce(jnp.maximum, beside_all, centre) - centre
    lower = reduce(jnp.minimum, beside_all, centre) - centre
    factor = jnp.ones_like(centre)
    for grad in grads:
        factor = jnp.minimum(factor, venkat(upper, lower, 0.5 * grad))
        factor = jnp.minimum(factor, venkat(upper, lower, -0.5 * grad))
    return (grads, [factor * grad for grad in grads])

def entropy_fix(speed):
    magnitude = jnp.abs(speed)
    return jnp.where(magnitude < FIX_WIDTH, (speed * speed + FIX_WIDTH * FIX_WIDTH) / (2.0 * FIX_WIDTH), magnitude)

def physical(state, direction):
    density = state[0]
    pressure = state[4]
    velocity = [state[1], state[2], state[3]]
    normal = velocity[direction]
    enthalpy = GAMMA / (GAMMA - 1.0) * pressure / density + 0.5 * (velocity[0] * velocity[0] + velocity[1] * velocity[1] + velocity[2] * velocity[2])
    moment = [density * velocity[comp] * normal + (pressure if comp == direction else 0.0) for comp in range(3)]
    return ([density * normal] + moment + [density * enthalpy * normal, density * state[5] * normal], enthalpy)

def roe_flux(left, right, direction):
    flux_left, enth_left = physical(left, direction)
    flux_right, enth_right = physical(right, direction)
    root_left = jnp.sqrt(left[0])
    root_right = jnp.sqrt(right[0])
    weight_left = root_left / (root_left + root_right)
    weight_right = root_right / (root_left + root_right)
    velocity = [weight_left * left[comp + 1] + weight_right * right[comp + 1] for comp in range(3)]
    enthalpy = weight_left * enth_left + weight_right * enth_right
    turbulent = weight_left * left[5] + weight_right * right[5]
    normal = velocity[direction]
    speed_sq = velocity[0] * velocity[0] + velocity[1] * velocity[1] + velocity[2] * velocity[2]
    sound_sq = (GAMMA - 1.0) * (enthalpy - 0.5 * speed_sq)
    sound = jnp.sqrt(sound_sq)
    dens_avg = root_left * root_right
    jump = right - left
    jump_vel = [jump[1], jump[2], jump[3]]
    jump_norm = jump_vel[direction]
    wave_slow = (jump[4] - dens_avg * sound * jump_norm) / (2.0 * sound_sq)
    wave_fast = (jump[4] + dens_avg * sound * jump_norm) / (2.0 * sound_sq)
    wave_mid = jump[0] - jump[4] / sound_sq
    slow = entropy_fix(normal - sound) * wave_slow
    middle = entropy_fix(normal)
    fast = entropy_fix(normal + sound) * wave_fast
    dissip = [slow + middle * wave_mid + fast]
    for comp in range(3):
        along = sound if comp == direction else 0.0
        shear = jump_vel[comp] - (jump_norm if comp == direction else 0.0)
        dissip.append(slow * (velocity[comp] - along) + middle * (wave_mid * velocity[comp] + dens_avg * shear) + fast * (velocity[comp] + along))
    inner = velocity[0] * jump_vel[0] + velocity[1] * jump_vel[1] + velocity[2] * jump_vel[2]
    dissip.append(slow * (enthalpy - sound * normal) + middle * (wave_mid * 0.5 * speed_sq + dens_avg * (inner - normal * jump_norm)) + fast * (enthalpy + sound * normal))
    dissip.append((slow + fast) * turbulent + middle * (wave_mid * turbulent + dens_avg * jump[5]))
    return jnp.stack([0.5 * (flux_left[comp] + flux_right[comp]) - 0.5 * dissip[comp] for comp in range(6)])

def divergence(line, slope, direction, axis):
    count = line.shape[axis] - 2
    left = lax.slice_in_dim(line, 0, count + 1, axis=axis) + 0.5 * lax.slice_in_dim(slope, 0, count + 1, axis=axis)
    right = lax.slice_in_dim(line, 1, count + 2, axis=axis) - 0.5 * lax.slice_in_dim(slope, 1, count + 2, axis=axis)
    flux = roe_flux(left, right, direction)
    return lax.slice_in_dim(flux, 1, count + 1, axis=axis) - lax.slice_in_dim(flux, 0, count, axis=axis)

def source_term(prim, grads, distance):
    omega_c = grads[1][3] - grads[2][2]
    omega_a = grads[2][1] - grads[0][3]
    omega_r = grads[0][2] - grads[1][1]
    vorticity = jnp.sqrt(omega_c * omega_c + omega_a * omega_a + omega_r * omega_r)
    ratio = prim[5] / distance
    return PRODUCE * vorticity * prim[0] * prim[5] - DESTROY * prim[0] * ratio * ratio

def pad_global(prim, inflow, wall_kind):
    extended = jnp.concatenate([prim[:, -1:], prim, prim[:, :1]], axis=1)
    entry_rows = jnp.concatenate([inflow[:, -1:], inflow, inflow[:, :1]], axis=1)[:, :, None, :]
    extended = jnp.concatenate([entry_rows, extended, extended[:, :, -1:]], axis=2)
    kinds = jnp.concatenate([wall_kind[:1], wall_kind, wall_kind[-1:]], axis=0)
    hub_ghost = reflect(extended[:, :, :, :1], kinds[:, 0])
    casing_ghost = reflect(extended[:, :, :, -1:], kinds[:, 1])
    return jnp.concatenate([hub_ghost, extended, casing_ghost], axis=3)

def residual(prim, inflow, wall_kind, distance):
    extended = pad_global(prim, inflow, wall_kind)
    grads, slopes = limited(extended)
    slope_circ = jnp.concatenate([slopes[0][:, -1:], slopes[0], slopes[0][:, :1]], axis=1)
    slope_axial = jnp.pad(slopes[1], ((0, 0), (0, 0), (1, 1), (0, 0)))
    slope_radial = jnp.pad(slopes[2], ((0, 0), (0, 0), (0, 0), (1, 1)))
    total = divergence(extended[:, :, 1:-1, 1:-1], slope_circ, 0, 1)
    total = total + divergence(extended[:, 1:-1, :, 1:-1], slope_axial, 1, 2)
    total = total + divergence(extended[:, 1:-1, 1:-1, :], slope_radial, 2, 3)
    source = source_term(prim, grads, distance)
    return jnp.concatenate([-total[:5], (-total[5] + source)[None]], axis=0)

def reference(flow, inflow, wall_kind):
    radial = jnp.arange(NR).astype(jnp.int32)
    distance = (jnp.minimum(radial, NR - 1 - radial) + 1).astype(jnp.float32)
    start = conserved(flow)
    section_one = start + STEP_SIZE * residual(flow, inflow, wall_kind, distance)
    section_two = section_one + STEP_SIZE * residual(primitive(section_one), inflow, wall_kind, distance)
    return 0.5 * start + 0.5 * section_two
```

```python
import jax
import jax.numpy as jnp
from jax import lax
from jax.experimental import pallas as pl
from jax.experimental.pallas import tpu as pltpu
from jax.sharding import PartitionSpec as P

MESH = pl.DeviceIdType.MESH
STEP_SIZE = 0.15
LIMIT_EPS = 0.03
FIX_WIDTH = 0.2
PRODUCE = 0.1355
DESTROY = 3.24

PLANES = 8
ROWS = 24

MESSAGES = (
    (1, 0, False, (4, 6), (8, 16), (0, 2), (8, 16)),
    (-1, 0, False, (2, 4), (8, 16), (6, 8), (8, 16)),
    (0, 1, False, (2, 6), (14, 16), (2, 6), (6, 8)),
    (0, -1, False, (2, 6), (8, 10), (2, 6), (16, 18)),
    (1, 1, False, (5, 6), (15, 16), (1, 2), (7, 8)),
    (1, -1, False, (5, 6), (8, 9), (1, 2), (16, 17)),
    (-1, 1, False, (2, 3), (15, 16), (6, 7), (7, 8)),
    (-1, -1, False, (2, 3), (8, 9), (6, 7), (16, 17)),
    (0, 0, True, (2, 6), (8, 16), (2, 6), (8, 16)),
    (1, 0, True, (5, 6), (8, 16), (1, 2), (8, 16)),
    (-1, 0, True, (2, 3), (8, 16), (6, 7), (8, 16)),
    (0, 1, True, (2, 6), (15, 16), (2, 6), (7, 8)),
    (0, -1, True, (2, 6), (8, 9), (2, 6), (16, 17)),
)
COUNT = len(MESSAGES)


def across(ref, m, row):
    return ref.at[pl.ds(m * PLANES * ROWS + row, 8, stride=ROWS), :]


def flat(ref):
    return ref.reshape(6 * PLANES * ROWS, 128)


def conserved(p):
    q = 0.5 * (p[1] * p[1] + p[2] * p[2] + p[3] * p[3])
    return [p[0], p[0] * p[1], p[0] * p[2], p[0] * p[3], 2.5 * p[4] + p[0] * q, p[0] * p[5]]


def primitive(u):
    inv = 1.0 / u[0]
    v = [u[1] * inv, u[2] * inv, u[3] * inv]
    pressure = 0.4 * (u[4] - 0.5 * u[0] * (v[0] * v[0] + v[1] * v[1] + v[2] * v[2]))
    return [u[0], v[0], v[1], v[2], pressure, u[5] * inv]


def limit(e, cp, cm, ap, am, rp, rm):
    dc, da, dr = cp - cm, ap - am, rp - rm
    top = jnp.maximum(jnp.maximum(jnp.maximum(cp, cm), jnp.maximum(ap, am)), jnp.maximum(jnp.maximum(rp, rm), e))
    low = jnp.minimum(jnp.minimum(jnp.minimum(cp, cm), jnp.minimum(ap, am)), jnp.minimum(jnp.minimum(rp, rm), e))
    bound = jnp.minimum(top - e, e - low)
    delta = 0.25 * jnp.maximum(jnp.maximum(jnp.abs(dc), jnp.abs(da)), jnp.abs(dr))
    square = bound * bound + LIMIT_EPS
    cross = bound * delta
    factor = jnp.minimum(1.0, (square + 2.0 * cross) / (square + cross + 2.0 * delta * delta))
    quarter = 0.25 * factor
    return (quarter * dc, quarter * da, quarter * dr), (dc, da, dr)


def fix(speed):
    size = jnp.abs(speed)
    return jnp.where(size < FIX_WIDTH, speed * speed * (0.5 / FIX_WIDTH) + 0.5 * FIX_WIDTH, size)


def side(s, d):
    y = lax.rsqrt(s[0])
    root = s[0] * y
    q = 0.5 * (s[1] * s[1] + s[2] * s[2] + s[3] * s[3])
    h = 3.5 * s[4] * (y * y) + q
    m = s[0] * s[d + 1]
    f = [m, m * s[1], m * s[2], m * s[3], m * h, m * s[5]]
    f[d + 1] = f[d + 1] + s[4]
    return root, h, f


def roe(left, right, d):
    rl, hl, fl = side(left, d)
    rr, hr, fr = side(right, d)
    jump = [r - l for l, r in zip(left, right)]
    w = rr / (rl + rr)
    vel = [left[k] + w * jump[k] for k in (1, 2, 3)]
    h = hl + w * (hr - hl)
    nu = left[5] + w * jump[5]
    un = vel[d]
    q = 0.5 * (vel[0] * vel[0] + vel[1] * vel[1] + vel[2] * vel[2])
    c2 = 0.4 * (h - q)
    ic = lax.rsqrt(c2)
    c = c2 * ic
    dens = rl * rr
    x = 0.5 * jump[4] * (ic * ic)
    y = 0.5 * dens * jump[d + 1] * ic
    mid = fix(un)
    slow = fix(un - c) * (x - y)
    fast = fix(un + c) * (x + y)
    both = slow + fast
    wave = mid * (jump[0] - 2.0 * x)
    total = both + wave
    skew = c * (fast - slow)
    shear = mid * dens
    dis = [total]
    inner = None
    for k in range(3):
        if k == d:
            dis.append(total * vel[k] + skew)
        else:
            part = shear * jump[k + 1]
            dis.append(total * vel[k] + part)
            inner = vel[k] * part if inner is None else inner + vel[k] * part
    dis.append(both * h + un * skew + wave * q + inner)
    dis.append(total * nu + shear * jump[5])
    return [fl[k] + fr[k] - dis[k] for k in range(6)]


def kernel(
    flow, inflow, walls, out,
    g1, g2, p1, p2, rs1, rs2, rr1, rr2, lc, rc, ap, am, lr, rr, src, fc, fa, fr, half, ns, entry, kinds,
    local_sem, send_sem, recv_sem, rad_send, rad_recv,
):
    ci, ai, ri = lax.axis_index("circ"), lax.axis_index("axial"), lax.axis_index("rad")
    nc, na = lax.axis_size("circ"), lax.axis_size("axial")
    other = 1 - ri
    first, last = ai == 0, ai == na - 1

    def target(dc, da, cross):
        return {"circ": lax.rem(ci + dc + nc, nc), "axial": ai + da, "rad": other if cross else ri}

    def there(da):
        return ai < na - 1 if da > 0 else ai > 0

    def guard(da, act):
        if da == 0:
            act()
        else:
            pl.when(there(da))(act)

    barrier = pltpu.get_barrier_semaphore()
    for dc, da, cross, *_ in MESSAGES:
        guard(da, lambda dc=dc, da=da, cross=cross: pl.semaphore_signal(
            barrier, inc=1, device_id=target(dc, da, cross), device_id_type=MESH))

    load = pltpu.make_async_copy(flow, g1.at[:, 2:6, 8:16, :], local_sem.at[0])
    load.start()
    lanes_from = pl.multiple_of(ri * 128, 128)
    enter = pltpu.make_async_copy(inflow.at[:, :, pl.ds(lanes_from, 128)], entry, local_sem.at[1])
    enter.start()
    kind = pltpu.make_async_copy(walls, kinds, local_sem.at[2])
    kind.start()
    load.wait()
    enter.wait()
    kind.wait()

    def message(phase, k):
        dc, da, cross, sp, sr, tp, tr = MESSAGES[k]
        own = (g1, g2)[phase]
        into = (p1, p2)[phase] if cross else own
        return pltpu.make_async_remote_copy(
            src_ref=own.at[:, sp[0]:sp[1], sr[0]:sr[1], :],
            dst_ref=into.at[:, tp[0]:tp[1], tr[0]:tr[1], :],
            send_sem=send_sem.at[phase, k],
            recv_sem=recv_sem.at[phase, k],
            device_id=target(dc, da, cross),
            device_id_type=MESH,
        )

    def send(phase):
        for k in range(COUNT):
            guard(MESSAGES[k][1], lambda k=k: message(phase, k).start())

    def receive(phase):
        for k in range(COUNT):
            guard(-MESSAGES[k][1], lambda k=k: message(phase, k).wait_recv())

    def sent(phase):
        for k in range(COUNT):
            guard(MESSAGES[k][1], lambda k=k: message(phase, k).wait_send())

    lane = lax.broadcasted_iota(jnp.int32, (8, 128), 1)
    at_first, at_last = lane == 0, lane == 127
    half_lane = jnp.where(lane >= 64, 1, 0)
    wall_lane = half_lane == 1 - ri
    wall_turn = jnp.where(ri == 0, 127, 1)
    radial = ri * 128 + lane
    wall_inv = 1.0 / (jnp.minimum(radial, 255 - radial) + 1).astype(jnp.float32)

    def ghost(e, beside, sign):
        return jnp.where(wall_lane, pltpu.roll(e * sign, wall_turn, 1), beside)

    def around(e, g):
        return pltpu.roll(jnp.where(at_first, g, e), 127, 1), pltpu.roll(jnp.where(at_last, g, e), 1, 1)

    for row in range(7, 17):
        station = jnp.clip(ai * 8 + (row - 8), 0, na * 8 - 1)
        value = jnp.where(kinds[ri, station] == 1, -1.0, 1.0)
        ns[pl.ds(row, 1), :] = jnp.full((1, 128), value, jnp.float32)

    def signs(tile):
        return (1.0, tile, tile, -1.0, 1.0, tile)

    def ends(own):
        @pl.when(first)
        def _():
            for m in range(6):
                for plane in range(1, 7):
                    at = lax.rem(ci * 4 + (plane - 2) + nc * 4, nc * 4)
                    own[m, plane, 7:8, :] = entry[m, pl.ds(at, 1), :]

        @pl.when(last)
        def _():
            for m in range(6):
                for plane in range(1, 7):
                    own[m, plane, 16:17, :] = own[m, plane, 15:16, :]

    def slopes(phase):
        own, beside = (g1, g2)[phase], (p1, p2)[phase]
        rs = (rs1, rs2)[phase]
        tile_sign = signs(ns[8:16, :])
        outward = jnp.where(ri == 0, 1.0, -1.0)

        def plane_step(c, carry):
            velocity = []
            for m in range(6):
                e = own[m, c, 8:16, :]
                g = ghost(e, beside[m, c, 8:16, :], tile_sign[m])
                rp, rm = around(e, g)
                hs, diff = limit(
                    e, own[m, c + 1, 8:16, :], own[m, c - 1, 8:16, :], own[m, c, 9:17, :], own[m, c, 7:15, :], rp, rm
                )
                velocity.append(diff)
                lc[m, c] = e + hs[0]
                rc[m, c] = e - hs[0]
                ap[m, c, 8:16, :] = e + hs[1]
                am[m, c, 8:16, :] = e - hs[1]
                lr[m, c] = e + hs[2]
                rr[m, c] = e - hs[2]
                rs[m, c] = e + outward * hs[2]
            oc = velocity[3][1] - velocity[2][2]
            oa = velocity[1][2] - velocity[3][0]
            orr = velocity[2][0] - velocity[1][1]
            s = jnp.sqrt(oc * oc + oa * oa + orr * orr)
            dens, nu = own[0, c, 8:16, :], own[5, c, 8:16, :]
            ratio = nu * wall_inv
            src[c] = (0.5 * PRODUCE) * s * dens * nu - DESTROY * dens * (ratio * ratio)
            return carry

        lax.fori_loop(1, 7, plane_step, 0)

        own_f, beside_f, ap_f, am_f = flat(own), flat(beside), flat(ap), flat(am)
        for row, held, step in ((7, first, 1.0), (16, last, -1.0)):
            row_sign = signs(jnp.broadcast_to(ns[row:row + 1, :], (8, 128)))
            for m in range(6):
                e = across(own_f, m, row)[...]
                g = ghost(e, across(beside_f, m, row)[...], row_sign[m])
                rp, rm = around(e, g)
                hs, _ = limit(
                    e, pltpu.roll(e, 7, 0), pltpu.roll(e, 1, 0), across(own_f, m, row + 1)[...],
                    across(own_f, m, row - 1)[...], rp, rm
                )
                into = across(ap_f if step > 0 else am_f, m, row)
                into[...] = e + jnp.where(held, 0.0, step * hs[1])

    def swap(phase):
        rs, rr_in = (rs1, rs2)[phase], (rr1, rr2)[phase]
        return pltpu.make_async_remote_copy(
            src_ref=rs.at[:, 2:6], dst_ref=rr_in, send_sem=rad_send.at[phase], recv_sem=rad_recv.at[phase],
            device_id={"circ": ci, "axial": ai, "rad": other}, device_id_type=MESH,
        )

    def faces():
        def circ_step(c, carry):
            f = roe([lc[m, c - 1] for m in range(6)], [rc[m, c] for m in range(6)], 0)
            for m in range(6):
                fc[m, c] = f[m]
            return carry

        lax.fori_loop(2, 7, circ_step, 0)

        def axial_step(c, carry):
            f = roe([ap[m, c, 7:15, :] for m in range(6)], [am[m, c, 8:16, :] for m in range(6)], 1)
            for m in range(6):
                fa[m, c, 8:16, :] = f[m]
            return carry

        lax.fori_loop(2, 6, axial_step, 0)
        ap_f, am_f, fa_f = flat(ap), flat(am), flat(fa)
        f = roe([across(ap_f, m, 15)[...] for m in range(6)], [across(am_f, m, 16)[...] for m in range(6)], 1)
        for m in range(6):
            across(fa_f, m, 16)[...] = f[m]

    def finish(phase):
        own, rr_in = (g1, g2)[phase], (rr1, rr2)[phase]
        tile_sign = signs(ns[8:16, :])
        pack_l = [jnp.full((8, 128), v, jnp.float32) for v in (1.0, 0.0, 0.0, 0.0, 1.0, 0.0)]
        pack_r = list(pack_l)
        for c in range(4):
            for m in range(6):
                g = ghost(own[m, c + 2, 8:16, :], rr_in[m, c], tile_sign[m])
                fr[m, c] = g
                pack_l[m] = jnp.where(lane == c, pltpu.roll(lr[m, c + 2], c + 1, 1), pack_l[m])
                pack_r[m] = jnp.where(lane == c, pltpu.roll(g, c, 1) if c else g, pack_r[m])
        extra = roe(pack_l, pack_r, 2)

        def step(c, carry):
            left = [pltpu.roll(jnp.where(at_last, fr[m, c], lr[m, c + 2]), 1, 1) for m in range(6)]
            f = roe(left, [rr[m, c + 2] for m in range(6)], 2)
            u0 = conserved([own[m, c + 2, 8:16, :] for m in range(6)])
            change = []
            for m in range(6):
                after = jnp.where(at_last, pltpu.roll(extra[m], 127 - c, 1), pltpu.roll(f[m], 127, 1))
                total = (
                    (fc[m, c + 3] - fc[m, c + 2])
                    + (fa[m, c + 2, 9:17, :] - fa[m, c + 2, 8:16, :])
                    + (after - f[m])
                )
                change.append((-0.5 * STEP_SIZE) * total)
            change[5] = change[5] + STEP_SIZE * src[c + 2]
            if phase == 0:
                u1 = [u0[m] + change[m] for m in range(6)]
                w = primitive(u1)
                for m in range(6):
                    g2[m, c + 2, 8:16, :] = w[m]
                    half[m, c] = 0.5 * (u0[m] + u1[m])
            else:
                for m in range(6):
                    out[m, c] = half[m, c] + 0.5 * change[m]
            return carry

        lax.fori_loop(0, 4, step, 0)

    pl.semaphore_wait(barrier, COUNT - 4 * first.astype(jnp.int32) - 4 * last.astype(jnp.int32))
    for phase in range(2):
        send(phase)
        receive(phase)
        ends((g1, g2)[phase])
        slopes(phase)
        swap(phase).start()
        faces()
        swap(phase).wait_recv()
        finish(phase)
    for phase in range(2):
        sent(phase)
        swap(phase).wait_send()


def solution(mesh):
    def vmem(*shape):
        return pltpu.VMEM(shape, jnp.float32)

    def body(flow, inflow, wall_kind):
        padded = (6, PLANES, ROWS, 128)
        tiles = (6, PLANES, 8, 128)
        inner = (6, 4, 8, 128)
        return pl.pallas_call(
            kernel,
            out_shape=jax.ShapeDtypeStruct(flow.shape, jnp.float32),
            in_specs=[pl.BlockSpec(memory_space=pl.ANY)] * 3,
            out_specs=pl.BlockSpec(memory_space=pltpu.VMEM),
            scratch_shapes=[
                vmem(*padded), vmem(*padded), vmem(*padded), vmem(*padded),
                vmem(*tiles), vmem(*tiles), vmem(*inner), vmem(*inner),
                vmem(*tiles), vmem(*tiles), vmem(*padded), vmem(*padded), vmem(*tiles), vmem(*tiles),
                vmem(PLANES, 8, 128), vmem(*tiles), vmem(*padded), vmem(*inner), vmem(*inner),
                vmem(ROWS, 128), vmem(6, inflow.shape[1], 128),
                pltpu.SMEM((2, wall_kind.shape[0]), jnp.int32),
                pltpu.SemaphoreType.DMA((3,)),
                pltpu.SemaphoreType.DMA((2, COUNT)), pltpu.SemaphoreType.DMA((2, COUNT)),
                pltpu.SemaphoreType.DMA((2,)), pltpu.SemaphoreType.DMA((2,)),
            ],
            compiler_params=pltpu.CompilerParams(
                collective_id=0, has_side_effects=True, vmem_limit_bytes=56 * 2**20
            ),
        )(flow, inflow, wall_kind.T)

    spec = P(None, "circ", "axial", "rad")
    return jax.shard_map(body, mesh=mesh, in_specs=(spec, P(), P()), out_specs=spec, check_vma=False)
```

```python
import jax
import jax.numpy as jnp
from jax import lax
from jax.experimental import pallas as pl
from jax.experimental.pallas import tpu as pltpu
from jax.sharding import PartitionSpec as P

MESH = pl.DeviceIdType.MESH
STEP_SIZE = 0.15
LIMIT_EPS = 0.03
FIX_WIDTH = 0.2
PRODUCE = 0.1355
DESTROY = 3.24

PLANES = 8
ROWS = 24

MESSAGES = (
    (0, 1, (2, 6), (14, 16), (2, 6), (6, 8)),
    (0, -1, (2, 6), (8, 10), (2, 6), (16, 18)),
    (1, 1, (5, 6), (15, 16), (1, 2), (7, 8)),
    (1, -1, (5, 6), (8, 9), (1, 2), (16, 17)),
    (-1, 1, (2, 3), (15, 16), (6, 7), (7, 8)),
    (-1, -1, (2, 3), (8, 9), (6, 7), (16, 17)),
    (1, 0, (4, 6), (8, 16), (0, 2), (8, 16)),
    (-1, 0, (2, 4), (8, 16), (6, 8), (8, 16)),
)
PACKED = (
    (0, 1, (0, 16)),
    (0, -1, (8, 24)),
    (1, 0, (8, 16)),
    (-1, 0, (8, 16)),
    (0, 0, (8, 16)),
)
FAR, BESIDE = len(MESSAGES), len(PACKED)


def slot(m, c):
    return 2 * (m * 6 + 1 + c)


def across(ref, phase, m, row, first=0, count=8):
    return ref.at[pl.ds(((phase * 6 + m) * PLANES + first) * ROWS + row, count, stride=ROWS), :]


def flat(ref):
    return ref.reshape(ref.size // 128, 128)


def conserved(p):
    q = 0.5 * (p[1] * p[1] + p[2] * p[2] + p[3] * p[3])
    return [p[0], p[0] * p[1], p[0] * p[2], p[0] * p[3], 2.5 * p[4] + p[0] * q, p[0] * p[5]]


def primitive(u):
    inv = 1.0 / u[0]
    v = [u[1] * inv, u[2] * inv, u[3] * inv]
    pressure = 0.4 * (u[4] - 0.5 * u[0] * (v[0] * v[0] + v[1] * v[1] + v[2] * v[2]))
    return [u[0], v[0], v[1], v[2], pressure, u[5] * inv]


def limit(e, cp, cm, ap, am, rp, rm):
    dc, da, dr = cp - cm, ap - am, rp - rm
    top = jnp.maximum(jnp.maximum(jnp.maximum(cp, cm), jnp.maximum(ap, am)), jnp.maximum(jnp.maximum(rp, rm), e))
    low = jnp.minimum(jnp.minimum(jnp.minimum(cp, cm), jnp.minimum(ap, am)), jnp.minimum(jnp.minimum(rp, rm), e))
    bound = jnp.minimum(top - e, e - low)
    delta = 0.25 * jnp.maximum(jnp.maximum(jnp.abs(dc), jnp.abs(da)), jnp.abs(dr))
    square = bound * bound + LIMIT_EPS
    cross = bound * delta
    factor = jnp.minimum(1.0, (square + 2.0 * cross) / (square + cross + 2.0 * delta * delta))
    quarter = 0.25 * factor
    return (quarter * dc, quarter * da, quarter * dr), (dc, da, dr)


def fix(speed):
    size = jnp.abs(speed)
    return jnp.where(size < FIX_WIDTH, speed * speed * (0.5 / FIX_WIDTH) + 0.5 * FIX_WIDTH, size)


def side(s, d):
    y = lax.rsqrt(s[0])
    root = s[0] * y
    q = 0.5 * (s[1] * s[1] + s[2] * s[2] + s[3] * s[3])
    h = 3.5 * s[4] * (y * y) + q
    m = s[0] * s[d + 1]
    f = [m, m * s[1], m * s[2], m * s[3], m * h, m * s[5]]
    f[d + 1] = f[d + 1] + s[4]
    return root, h, f


def roe(left, right, d):
    rl, hl, fl = side(left, d)
    rr, hr, fr = side(right, d)
    jump = [r - l for l, r in zip(left, right)]
    w = rr / (rl + rr)
    vel = [left[k] + w * jump[k] for k in (1, 2, 3)]
    h = hl + w * (hr - hl)
    nu = left[5] + w * jump[5]
    un = vel[d]
    q = 0.5 * (vel[0] * vel[0] + vel[1] * vel[1] + vel[2] * vel[2])
    c2 = 0.4 * (h - q)
    ic = lax.rsqrt(c2)
    c = c2 * ic
    dens = rl * rr
    x = 0.5 * jump[4] * (ic * ic)
    y = 0.5 * dens * jump[d + 1] * ic
    mid = fix(un)
    slow = fix(un - c) * (x - y)
    fast = fix(un + c) * (x + y)
    both = slow + fast
    wave = mid * (jump[0] - 2.0 * x)
    total = both + wave
    skew = c * (fast - slow)
    shear = mid * dens
    dis = [total]
    inner = None
    for k in range(3):
        if k == d:
            dis.append(total * vel[k] + skew)
        else:
            part = shear * jump[k + 1]
            dis.append(total * vel[k] + part)
            inner = vel[k] * part if inner is None else inner + vel[k] * part
    dis.append(both * h + un * skew + wave * q + inner)
    dis.append(total * nu + shear * jump[5])
    return [fl[k] + fr[k] - dis[k] for k in range(6)]


def kernel(
    flow, inflow, walls, out,
    g, pack, land, packed, edge, lc, rc, ap, am, lr, rr, src, fa, ns, entry, entry_packed, kinds,
    local_sem, send_sem, recv_sem,
):
    ci, ai, ri = lax.axis_index("circ"), lax.axis_index("axial"), lax.axis_index("rad")
    nc, na = lax.axis_size("circ"), lax.axis_size("axial")
    first, last = ai == 0, ai == na - 1

    def target(dc, da, cross):
        return {"circ": lax.rem(ci + dc + nc, nc), "axial": ai + da, "rad": 1 - ri if cross else ri}

    def there(da):
        return ai < na - 1 if da > 0 else ai > 0

    def guard(da, act):
        if da == 0:
            act()
        else:
            pl.when(there(da))(act)

    barrier = pltpu.get_barrier_semaphore()
    for cross, group in ((False, MESSAGES), (True, PACKED)):
        for dc, da, *_ in group:
            guard(da, lambda dc=dc, da=da, cross=cross: pl.semaphore_signal(
                barrier, inc=1, device_id=target(dc, da, cross), device_id_type=MESH))

    load = pltpu.make_async_copy(flow, g.at[0, :, 2:6, 8:16, :], local_sem.at[0])
    load.start()
    kind = pltpu.make_async_copy(walls, kinds, local_sem.at[1])
    kind.start()
    enter = [
        pltpu.make_async_copy(
            inflow.at[:, :, pl.ds(pl.multiple_of(core * 128, 128), 128)], entry.at[k], local_sem.at[2 + k])
        for k, core in enumerate((ri, 1 - ri))
    ]
    for part in enter:
        part.start()

    def far(phase, k):
        dc, da, sp, sr, tp, tr = MESSAGES[k]
        return pltpu.make_async_remote_copy(
            src_ref=g.at[phase, :, sp[0]:sp[1], sr[0]:sr[1], :],
            dst_ref=g.at[phase, :, tp[0]:tp[1], tr[0]:tr[1], :],
            send_sem=send_sem.at[phase, k],
            recv_sem=recv_sem.at[phase, k],
            device_id=target(dc, da, False),
            device_id_type=MESH,
        )

    def beside(phase, k):
        dc, da, rows = PACKED[k]
        return pltpu.make_async_remote_copy(
            src_ref=pack.at[phase, rows[0]:rows[1], :],
            dst_ref=land.at[phase, k, rows[0]:rows[1], :],
            send_sem=send_sem.at[phase, FAR + k],
            recv_sem=recv_sem.at[phase, FAR + k],
            device_id=target(dc, da, True),
            device_id_type=MESH,
        )

    def each(group, act, back, wanted):
        for k, (dc, da, *_) in enumerate(group):
            if (da != 0) in wanted:
                guard(-da if back else da, lambda k=k: act(k))

    lane = lax.broadcasted_iota(jnp.int32, (8, 128), 1)
    at_first, at_last = lane == 0, lane == 127
    hub_lane, casing_lane = lane + 128 * ri == 0, lane + 128 * ri == 255
    radial = ri * 128 + lane
    wall_inv = 1.0 / (jnp.minimum(radial, 255 - radial) + 1).astype(jnp.float32)
    inner_turn = jnp.where(ri == 0, 127, 1)

    def around(e, near, sign):
        mirror = e * sign
        after = pltpu.roll(jnp.where(at_first, near, e), 127, 1)
        before = pltpu.roll(jnp.where(at_last, near, e), 1, 1)
        return jnp.where(casing_lane, mirror, after), jnp.where(hub_lane, mirror, before)

    def signs(tile):
        return (1.0, tile, tile, -1.0, 1.0, tile)

    def fill(phase):
        tile = jnp.zeros((8, 128), jnp.float32)
        for m in range(6):
            for c in range(4):
                at = slot(m, c)
                e = g[phase, m, c + 2, 8:16, :]
                turned = pltpu.roll(e, jnp.where(ri == 0, (at + 2) % 128, at), 1)
                tile = jnp.where((lane == at) | (lane == at + 1), turned, tile)
        pack[phase, 8:16, :] = tile
        for row, start in ((15, 0), (8, 16)):
            tile = jnp.zeros((4, 128), jnp.float32)
            for m in range(6):
                e = across(flat(g), phase, m, row, 2, 4)[...]
                here = lane[0:4] == lax.rem(m + 127 * (1 - ri), 128)
                tile = jnp.where(here, pltpu.roll(e, m, 1) if m else e, tile)
            pack[phase, start:start + 4, :] = tile

    def station_signs():
        for row in range(7, 17):
            station = jnp.clip(ai * 8 + (row - 8), 0, na * 8 - 1)
            value = jnp.where(kinds[ri, station] == 1, -1.0, 1.0)
            ns[pl.ds(row, 1), :] = jnp.full((1, 128), value, jnp.float32)

    def entry_rows():
        row = jnp.zeros((1, 128), jnp.float32)
        for m in range(6):
            for plane in range(1, 7):
                at = lax.rem(ci * 4 + (plane - 2) + nc * 4, nc * 4)
                mine = entry[0, m, pl.ds(at, 1), :]
                for phase in range(2):
                    g[phase, m, plane, 7:8, :] = mine
                if 2 <= plane < 6:
                    theirs = entry[1, m, pl.ds(at, 1), :]
                    k = slot(m, plane - 2)
                    turned = pltpu.roll(
                        jnp.broadcast_to(theirs, (8, 128)), jnp.where(ri == 0, k, (k + 2) % 128), 1)[0:1]
                    row = jnp.where((lane[0:1] == k) | (lane[0:1] == k + 1), turned, row)
        entry_packed[0:1, :] = row

    def section(phase, carry):
        each(MESSAGES, lambda k: far(phase, k).start(), False, (True,))
        each(PACKED, lambda k: beside(phase, k).start(), False, (True, False))
        each(MESSAGES, lambda k: far(phase, k).start(), False, (False,))
        each(PACKED, lambda k: beside(phase, k).wait_recv(), True, (False,))
        each(MESSAGES, lambda k: far(phase, k).wait_recv(), True, (False,))

        place = lax.rem(lane // 2, 6)
        halo = jnp.where(place == 0, pltpu.roll(land[phase, 2, 8:16, :], 120, 1), land[phase, 4, 8:16, :])
        halo = jnp.where(place == 5, pltpu.roll(land[phase, 3, 8:16, :], 8, 1), halo)
        packed[8:16, :] = halo
        turned = pltpu.roll(halo, jnp.where(ri == 0, 0, 126), 1)
        for c in range(-1, 5):
            for m in range(6):
                edge[m, c + 2] = pltpu.roll(turned, (128 - slot(m, c)) % 128, 1)

        each(PACKED, lambda k: beside(phase, k).wait_recv(), True, (True,))
        each(MESSAGES, lambda k: far(phase, k).wait_recv(), True, (True,))

        @pl.when(first)
        def _():
            packed[7:8, :] = entry_packed[0:1, :]

        @pl.when(jnp.logical_not(first))
        def _():
            packed[7:8, :] = land[phase, 0, 15:16, :]

        @pl.when(last)
        def _():
            packed[16:17, :] = packed[15:16, :]
            for m in range(6):
                for plane in range(1, 7):
                    g[phase, m, plane, 16:17, :] = g[phase, m, plane, 15:16, :]

        @pl.when(jnp.logical_not(last))
        def _():
            packed[16:17, :] = land[phase, 1, 8:9, :]

        z = packed[8:16, :]
        beyond, mine = pltpu.roll(z, inner_turn, 1), pltpu.roll(pack[phase, 8:16, :], inner_turn, 1)
        hs, _ = limit(
            z, pltpu.roll(z, 126, 1), pltpu.roll(z, 2, 1), packed[9:17, :], packed[7:15, :], beyond, mine
        )
        near_face = pltpu.roll(z - hs[2], jnp.where(ri == 0, 0, 126), 1)

        tile_sign = signs(ns[8:16, :])
        for c in range(1, 7):
            diffs = []
            for m in range(6):
                e = g[phase, m, c, 8:16, :]
                rp, rm = around(e, edge[m, c], tile_sign[m])
                hs, diff = limit(
                    e, g[phase, m, c + 1, 8:16, :], g[phase, m, c - 1, 8:16, :],
                    g[phase, m, c, 9:17, :], g[phase, m, c, 7:15, :], rp, rm
                )
                diffs.append(diff)
                lc[m, c] = e + hs[0]
                rc[m, c] = e - hs[0]
                if 2 <= c < 6:
                    ap[m, c, 8:16, :] = e + hs[1]
                    am[m, c, 8:16, :] = e - hs[1]
                    lr[m, c - 2] = e + hs[2]
                    rr[m, c - 2] = e - hs[2]
            if 2 <= c < 6:
                oc = diffs[3][1] - diffs[2][2]
                oa = diffs[1][2] - diffs[3][0]
                orr = diffs[2][0] - diffs[1][1]
                s = jnp.sqrt(oc * oc + oa * oa + orr * orr)
                dens, nu = g[phase, 0, c, 8:16, :], g[phase, 5, c, 8:16, :]
                ratio = nu * wall_inv
                src[c - 2] = (0.5 * PRODUCE) * s * dens * nu - DESTROY * dens * (ratio * ratio)

        g_f, ap_f, am_f, fa_f = flat(g), flat(ap), flat(am), flat(fa)
        for k, row, held, step in ((0, 7, first, 1.0), (1, 16, last, -1.0)):
            row_sign = signs(jnp.broadcast_to(ns[row:row + 1, :], (8, 128)))
            columns = pltpu.roll(land[phase, k, (0, 16)[k]:(8, 24)[k], :], 2, 0)
            for m in range(6):
                e = across(g_f, phase, m, row)[...]
                rp, rm = around(e, pltpu.roll(columns, 128 - m, 1) if m else columns, row_sign[m])
                hs, _ = limit(
                    e, pltpu.roll(e, 7, 0), pltpu.roll(e, 1, 0), across(g_f, phase, m, row + 1)[...],
                    across(g_f, phase, m, row - 1)[...], rp, rm
                )
                across(ap_f if step > 0 else am_f, 0, m, row)[...] = e + jnp.where(held, 0.0, step * hs[1])

        for c in range(2, 6):
            f = roe([ap[m, c, 7:15, :] for m in range(6)], [am[m, c, 8:16, :] for m in range(6)], 1)
            for m in range(6):
                fa[m, c, 8:16, :] = f[m]
        f = roe([across(ap_f, 0, m, 15)[...] for m in range(6)], [across(am_f, 0, m, 16)[...] for m in range(6)], 1)
        for m in range(6):
            across(fa_f, 0, m, 16)[...] = f[m]

        pack_l = [jnp.full((8, 128), v, jnp.float32) for v in (1.0, 0.0, 0.0, 0.0, 1.0, 0.0)]
        pack_r = list(pack_l)
        nears = []
        for c in range(4):
            nears.append([])
            for m in range(6):
                near = pltpu.roll(near_face, (128 - slot(m, c)) % 128, 1)
                nears[c].append(near)
                e = g[phase, m, c + 2, 8:16, :] * tile_sign[m]
                wall = pltpu.roll(e, c + 1, 1)
                pack_l[m] = jnp.where(lane == c, pltpu.roll(lr[m, c], c + 1, 1), pack_l[m])
                after = jnp.where(ri == 0, pltpu.roll(near, c, 1) if c else near, wall)
                pack_r[m] = jnp.where(lane == c, after, pack_r[m])
        extra = roe(pack_l, pack_r, 2)

        fc = roe([lc[m, 1] for m in range(6)], [rc[m, 2] for m in range(6)], 0)
        for c in range(4):
            fc_next = roe([lc[m, c + 2] for m in range(6)], [rc[m, c + 3] for m in range(6)], 0)
            e = [g[phase, m, c + 2, 8:16, :] for m in range(6)]
            left = [
                jnp.where(
                    hub_lane, e[m] * tile_sign[m], pltpu.roll(jnp.where(at_last, nears[c][m], lr[m, c]), 1, 1)
                )
                for m in range(6)
            ]
            fr = roe(left, [rr[m, c] for m in range(6)], 2)
            u0 = conserved(e)
            u1 = []
            for m in range(6):
                after = jnp.where(at_last, pltpu.roll(extra[m], 127 - c, 1), pltpu.roll(fr[m], 127, 1))
                total = (
                    (fc_next[m] - fc[m])
                    + (fa[m, c + 2, 9:17, :] - fa[m, c + 2, 8:16, :])
                    + (after - fr[m])
                )
                change = (-0.5 * STEP_SIZE) * total
                if m == 5:
                    change = change + STEP_SIZE * src[c]
                u1.append(u0[m] + change)
                out[m, c] = jnp.where(phase == 0, u0[m], out[m, c]) + 0.5 * change
            w = primitive(u1)
            for m in range(6):
                g[phase + 1, m, c + 2, 8:16, :] = w[m]
            fc = fc_next
        fill(phase + 1)
        return carry

    load.wait()
    kind.wait()
    for part in enter:
        part.wait()
    station_signs()
    pl.when(first)(entry_rows)
    fill(0)
    pl.semaphore_wait(barrier, FAR + BESIDE - 4 * first.astype(jnp.int32) - 4 * last.astype(jnp.int32))
    lax.fori_loop(0, 2, section, 0)
    for phase in range(2):
        each(MESSAGES, lambda k: far(phase, k).wait_send(), False, (True, False))
        each(PACKED, lambda k: beside(phase, k).wait_send(), False, (True, False))


def solution(mesh):
    def vmem(*shape):
        return pltpu.VMEM(shape, jnp.float32)

    def body(flow, inflow, wall_kind):
        padded = (6, PLANES, ROWS, 128)
        tiles = (6, PLANES, 8, 128)
        inner = (6, 4, 8, 128)
        return pl.pallas_call(
            kernel,
            out_shape=jax.ShapeDtypeStruct(flow.shape, jnp.float32),
            in_specs=[pl.BlockSpec(memory_space=pl.ANY)] * 3,
            out_specs=pl.BlockSpec(memory_space=pltpu.VMEM),
            scratch_shapes=[
                vmem(3, *padded), vmem(3, 24, 128), vmem(2, BESIDE, 24, 128), vmem(24, 128),
                vmem(*tiles), vmem(*tiles), vmem(*tiles), vmem(*padded), vmem(*padded), vmem(*inner), vmem(*inner),
                vmem(4, 8, 128), vmem(*padded), vmem(ROWS, 128), vmem(2, 6, inflow.shape[1], 128), vmem(8, 128),
                pltpu.SMEM((2, wall_kind.shape[0]), jnp.int32),
                pltpu.SemaphoreType.DMA((4,)),
                pltpu.SemaphoreType.DMA((2, FAR + BESIDE)), pltpu.SemaphoreType.DMA((2, FAR + BESIDE)),
            ],
            compiler_params=pltpu.CompilerParams(
                collective_id=0, has_side_effects=True, vmem_limit_bytes=56 * 2**20
            ),
        )(flow, inflow, wall_kind.T)

    spec = P(None, "circ", "axial", "rad")
    return jax.shard_map(body, mesh=mesh, in_specs=(spec, P(), P()), out_specs=spec, check_vma=False)
```

```python
import jax
import jax.numpy as jnp
from jax import lax
from jax.experimental import pallas as pl
from jax.experimental.pallas import tpu as pltpu
from jax.sharding import PartitionSpec as P

MESH = pl.DeviceIdType.MESH
STEP_SIZE = 0.15
LIMIT_EPS = 0.03
FIX_WIDTH = 0.2
PRODUCE = 0.1355
DESTROY = 3.24

PLANES = 8
ROWS = 24

MESSAGES = (
    (0, 1, (2, 6), (14, 16), (2, 6), (6, 8)),
    (0, -1, (2, 6), (8, 10), (2, 6), (16, 18)),
    (1, 1, (5, 6), (15, 16), (1, 2), (7, 8)),
    (1, -1, (5, 6), (8, 9), (1, 2), (16, 17)),
    (-1, 1, (2, 3), (15, 16), (6, 7), (7, 8)),
    (-1, -1, (2, 3), (8, 9), (6, 7), (16, 17)),
    (1, 0, (4, 6), (8, 16), (0, 2), (8, 16)),
    (-1, 0, (2, 4), (8, 16), (6, 8), (8, 16)),
)
PACKED = (
    (0, 1, (0, 16)),
    (0, -1, (8, 24)),
    (1, 0, (8, 16)),
    (-1, 0, (8, 16)),
    (0, 0, (8, 16)),
)
FAR, BESIDE = len(MESSAGES), len(PACKED)


def slot(m, c):
    return 2 * (m * 6 + 1 + c)


def across(ref, phase, m, row, first=0, count=8):
    return ref.at[pl.ds(((phase * 6 + m) * PLANES + first) * ROWS + row, count, stride=ROWS), :]


def flat(ref):
    return ref.reshape(ref.size // 128, 128)


def conserved(p):
    q = 0.5 * (p[1] * p[1] + p[2] * p[2] + p[3] * p[3])
    return [p[0], p[0] * p[1], p[0] * p[2], p[0] * p[3], 2.5 * p[4] + p[0] * q, p[0] * p[5]]


def primitive(u):
    inv = 1.0 / u[0]
    v = [u[1] * inv, u[2] * inv, u[3] * inv]
    pressure = 0.4 * (u[4] - 0.5 * u[0] * (v[0] * v[0] + v[1] * v[1] + v[2] * v[2]))
    return [u[0], v[0], v[1], v[2], pressure, u[5] * inv]


def limit(e, cp, cm, ap, am, rp, rm):
    dc, da, dr = cp - cm, ap - am, rp - rm
    top = jnp.maximum(jnp.maximum(jnp.maximum(cp, cm), jnp.maximum(ap, am)), jnp.maximum(jnp.maximum(rp, rm), e))
    low = jnp.minimum(jnp.minimum(jnp.minimum(cp, cm), jnp.minimum(ap, am)), jnp.minimum(jnp.minimum(rp, rm), e))
    bound = jnp.minimum(top - e, e - low)
    delta = 0.25 * jnp.maximum(jnp.maximum(jnp.abs(dc), jnp.abs(da)), jnp.abs(dr))
    square = bound * bound + LIMIT_EPS
    cross = bound * delta
    factor = jnp.minimum(1.0, (square + 2.0 * cross) / (square + cross + 2.0 * delta * delta))
    quarter = 0.25 * factor
    return (quarter * dc, quarter * da, quarter * dr), (dc, da, dr)


def fix(speed):
    size = jnp.abs(speed)
    return jnp.where(size < FIX_WIDTH, speed * speed * (0.5 / FIX_WIDTH) + 0.5 * FIX_WIDTH, size)


def side(s, d):
    y = lax.rsqrt(s[0])
    root = s[0] * y
    q = 0.5 * (s[1] * s[1] + s[2] * s[2] + s[3] * s[3])
    h = 3.5 * s[4] * (y * y) + q
    m = s[0] * s[d + 1]
    f = [m, m * s[1], m * s[2], m * s[3], m * h, m * s[5]]
    f[d + 1] = f[d + 1] + s[4]
    return root, h, f


def roe(left, right, d):
    rl, hl, fl = side(left, d)
    rr, hr, fr = side(right, d)
    jump = [r - l for l, r in zip(left, right)]
    w = rr / (rl + rr)
    vel = [left[k] + w * jump[k] for k in (1, 2, 3)]
    h = hl + w * (hr - hl)
    nu = left[5] + w * jump[5]
    un = vel[d]
    q = 0.5 * (vel[0] * vel[0] + vel[1] * vel[1] + vel[2] * vel[2])
    c2 = 0.4 * (h - q)
    ic = lax.rsqrt(c2)
    c = c2 * ic
    dens = rl * rr
    x = 0.5 * jump[4] * (ic * ic)
    y = 0.5 * dens * jump[d + 1] * ic
    mid = fix(un)
    slow = fix(un - c) * (x - y)
    fast = fix(un + c) * (x + y)
    both = slow + fast
    wave = mid * (jump[0] - 2.0 * x)
    total = both + wave
    skew = c * (fast - slow)
    shear = mid * dens
    dis = [total]
    inner = None
    for k in range(3):
        if k == d:
            dis.append(total * vel[k] + skew)
        else:
            part = shear * jump[k + 1]
            dis.append(total * vel[k] + part)
            inner = vel[k] * part if inner is None else inner + vel[k] * part
    dis.append(both * h + un * skew + wave * q + inner)
    dis.append(total * nu + shear * jump[5])
    return [fl[k] + fr[k] - dis[k] for k in range(6)]


def kernel(
    flow, inflow, walls, out,
    g, pack, land, packed, edge, lc, rc, ap, am, lr, rr, src, fa, ns, entry, entry_packed, kinds,
    local_sem, send_sem, recv_sem,
):
    ci, ai, ri = lax.axis_index("circ"), lax.axis_index("axial"), lax.axis_index("rad")
    nc, na = lax.axis_size("circ"), lax.axis_size("axial")
    first, last = ai == 0, ai == na - 1

    def target(dc, da, cross):
        return {"circ": lax.rem(ci + dc + nc, nc), "axial": ai + da, "rad": 1 - ri if cross else ri}

    def there(da):
        return ai < na - 1 if da > 0 else ai > 0

    def guard(da, act):
        if da == 0:
            act()
        else:
            pl.when(there(da))(act)

    barrier = pltpu.get_barrier_semaphore()
    for cross, group in ((False, MESSAGES), (True, PACKED)):
        for dc, da, *_ in group:
            guard(da, lambda dc=dc, da=da, cross=cross: pl.semaphore_signal(
                barrier, inc=1, device_id=target(dc, da, cross), device_id_type=MESH))

    load = pltpu.make_async_copy(flow, g.at[0, :, 2:6, 8:16, :], local_sem.at[0])
    load.start()
    kind = pltpu.make_async_copy(walls, kinds, local_sem.at[1])
    kind.start()
    enter = [
        pltpu.make_async_copy(
            inflow.at[:, :, pl.ds(pl.multiple_of(core * 128, 128), 128)], entry.at[k], local_sem.at[2 + k])
        for k, core in enumerate((ri, 1 - ri))
    ]
    for part in enter:
        part.start()

    def far(phase, k):
        dc, da, sp, sr, tp, tr = MESSAGES[k]
        return pltpu.make_async_remote_copy(
            src_ref=g.at[phase, :, sp[0]:sp[1], sr[0]:sr[1], :],
            dst_ref=g.at[phase, :, tp[0]:tp[1], tr[0]:tr[1], :],
            send_sem=send_sem.at[phase, k],
            recv_sem=recv_sem.at[phase, k],
            device_id=target(dc, da, False),
            device_id_type=MESH,
        )

    def beside(phase, k):
        dc, da, rows = PACKED[k]
        return pltpu.make_async_remote_copy(
            src_ref=pack.at[phase, rows[0]:rows[1], :],
            dst_ref=land.at[phase, k, rows[0]:rows[1], :],
            send_sem=send_sem.at[phase, FAR + k],
            recv_sem=recv_sem.at[phase, FAR + k],
            device_id=target(dc, da, True),
            device_id_type=MESH,
        )

    def each(group, act, back, wanted):
        for k, (dc, da, *_) in enumerate(group):
            if (da != 0) in wanted:
                guard(-da if back else da, lambda k=k: act(k))

    lane = lax.broadcasted_iota(jnp.int32, (8, 128), 1)
    at_first, at_last = lane == 0, lane == 127
    hub_lane, casing_lane = lane + 128 * ri == 0, lane + 128 * ri == 255
    radial = ri * 128 + lane
    wall_inv = 1.0 / (jnp.minimum(radial, 255 - radial) + 1).astype(jnp.float32)
    inner_turn = jnp.where(ri == 0, 127, 1)

    def around(e, near, sign):
        mirror = e * sign
        after = pltpu.roll(jnp.where(at_first, near, e), 127, 1)
        before = pltpu.roll(jnp.where(at_last, near, e), 1, 1)
        return jnp.where(casing_lane, mirror, after), jnp.where(hub_lane, mirror, before)

    def signs(tile):
        return (1.0, tile, tile, -1.0, 1.0, tile)

    def fill(phase):
        tile = jnp.zeros((8, 128), jnp.float32)
        for m in range(6):
            for c in range(4):
                at = slot(m, c)
                e = g[phase, m, c + 2, 8:16, :]
                turned = pltpu.roll(e, jnp.where(ri == 0, (at + 2) % 128, at), 1)
                tile = jnp.where((lane == at) | (lane == at + 1), turned, tile)
        pack[phase, 8:16, :] = tile
        for row, start in ((15, 0), (8, 16)):
            tile = jnp.zeros((4, 128), jnp.float32)
            for m in range(6):
                e = across(flat(g), phase, m, row, 2, 4)[...]
                here = lane[0:4] == lax.rem(m + 127 * (1 - ri), 128)
                tile = jnp.where(here, pltpu.roll(e, m, 1) if m else e, tile)
            pack[phase, start:start + 4, :] = tile

    def station_signs():
        for row in range(7, 17):
            station = jnp.clip(ai * 8 + (row - 8), 0, na * 8 - 1)
            value = jnp.where(kinds[ri, station] == 1, -1.0, 1.0)
            ns[pl.ds(row, 1), :] = jnp.full((1, 128), value, jnp.float32)

    def entry_rows():
        row = jnp.zeros((1, 128), jnp.float32)
        for m in range(6):
            for plane in range(1, 7):
                at = lax.rem(ci * 4 + (plane - 2) + nc * 4, nc * 4)
                mine = entry[0, m, pl.ds(at, 1), :]
                for phase in range(2):
                    g[phase, m, plane, 7:8, :] = mine
                if 2 <= plane < 6:
                    theirs = entry[1, m, pl.ds(at, 1), :]
                    k = slot(m, plane - 2)
                    turned = pltpu.roll(
                        jnp.broadcast_to(theirs, (8, 128)), jnp.where(ri == 0, k, (k + 2) % 128), 1)[0:1]
                    row = jnp.where((lane[0:1] == k) | (lane[0:1] == k + 1), turned, row)
        entry_packed[0:1, :] = row

    def section(phase, carry):
        each(MESSAGES, lambda k: far(phase, k).start(), False, (True,))
        each(PACKED, lambda k: beside(phase, k).start(), False, (True, False))
        each(MESSAGES, lambda k: far(phase, k).start(), False, (False,))
        each(PACKED, lambda k: beside(phase, k).wait_recv(), True, (False,))
        each(MESSAGES, lambda k: far(phase, k).wait_recv(), True, (False,))

        place = lax.rem(lane // 2, 6)
        halo = jnp.where(place == 0, pltpu.roll(land[phase, 2, 8:16, :], 120, 1), land[phase, 4, 8:16, :])
        halo = jnp.where(place == 5, pltpu.roll(land[phase, 3, 8:16, :], 8, 1), halo)
        packed[8:16, :] = halo
        turned = pltpu.roll(halo, jnp.where(ri == 0, 0, 126), 1)
        for c in range(-1, 5):
            for m in range(6):
                edge[m, c + 2] = pltpu.roll(turned, (128 - slot(m, c)) % 128, 1)

        each(PACKED, lambda k: beside(phase, k).wait_recv(), True, (True,))
        each(MESSAGES, lambda k: far(phase, k).wait_recv(), True, (True,))

        @pl.when(first)
        def _():
            packed[7:8, :] = entry_packed[0:1, :]

        @pl.when(jnp.logical_not(first))
        def _():
            packed[7:8, :] = land[phase, 0, 15:16, :]

        @pl.when(last)
        def _():
            packed[16:17, :] = packed[15:16, :]
            for m in range(6):
                for plane in range(1, 7):
                    g[phase, m, plane, 16:17, :] = g[phase, m, plane, 15:16, :]

        @pl.when(jnp.logical_not(last))
        def _():
            packed[16:17, :] = land[phase, 1, 8:9, :]

        z = packed[8:16, :]
        beyond, mine = pltpu.roll(z, inner_turn, 1), pltpu.roll(pack[phase, 8:16, :], inner_turn, 1)
        hs, _ = limit(
            z, pltpu.roll(z, 126, 1), pltpu.roll(z, 2, 1), packed[9:17, :], packed[7:15, :], beyond, mine
        )
        near_face = pltpu.roll(z - hs[2], jnp.where(ri == 0, 0, 126), 1)

        tile_sign = signs(ns[8:16, :])
        for c in range(1, 7):
            diffs = []
            for m in range(6):
                e = g[phase, m, c, 8:16, :]
                rp, rm = around(e, edge[m, c], tile_sign[m])
                hs, diff = limit(
                    e, g[phase, m, c + 1, 8:16, :], g[phase, m, c - 1, 8:16, :],
                    g[phase, m, c, 9:17, :], g[phase, m, c, 7:15, :], rp, rm
                )
                diffs.append(diff)
                lc[m, c] = e + hs[0]
                rc[m, c] = e - hs[0]
                if 2 <= c < 6:
                    ap[m, c, 8:16, :] = e + hs[1]
                    am[m, c, 8:16, :] = e - hs[1]
                    lr[m, c - 2] = e + hs[2]
                    rr[m, c - 2] = e - hs[2]
            if 2 <= c < 6:
                oc = diffs[3][1] - diffs[2][2]
                oa = diffs[1][2] - diffs[3][0]
                orr = diffs[2][0] - diffs[1][1]
                s = jnp.sqrt(oc * oc + oa * oa + orr * orr)
                dens, nu = g[phase, 0, c, 8:16, :], g[phase, 5, c, 8:16, :]
                ratio = nu * wall_inv
                src[c - 2] = (0.5 * PRODUCE) * s * dens * nu - DESTROY * dens * (ratio * ratio)

        g_f, ap_f, am_f, fa_f = flat(g), flat(ap), flat(am), flat(fa)
        for k, row, held, step in ((0, 7, first, 1.0), (1, 16, last, -1.0)):
            row_sign = signs(jnp.broadcast_to(ns[row:row + 1, :], (8, 128)))
            columns = pltpu.roll(land[phase, k, (0, 16)[k]:(8, 24)[k], :], 2, 0)
            for m in range(6):
                e = across(g_f, phase, m, row)[...]
                rp, rm = around(e, pltpu.roll(columns, 128 - m, 1) if m else columns, row_sign[m])
                hs, _ = limit(
                    e, pltpu.roll(e, 7, 0), pltpu.roll(e, 1, 0), across(g_f, phase, m, row + 1)[...],
                    across(g_f, phase, m, row - 1)[...], rp, rm
                )
                across(ap_f if step > 0 else am_f, 0, m, row)[...] = e + jnp.where(held, 0.0, step * hs[1])

        for c in range(2, 6):
            f = roe([ap[m, c, 7:15, :] for m in range(6)], [am[m, c, 8:16, :] for m in range(6)], 1)
            for m in range(6):
                fa[m, c, 8:16, :] = f[m]
        f = roe([across(ap_f, 0, m, 15)[...] for m in range(6)], [across(am_f, 0, m, 16)[...] for m in range(6)], 1)
        for m in range(6):
            across(fa_f, 0, m, 16)[...] = f[m]

        pack_l = [jnp.full((8, 128), v, jnp.float32) for v in (1.0, 0.0, 0.0, 0.0, 1.0, 0.0)]
        pack_r = list(pack_l)
        nears = []
        for c in range(4):
            nears.append([])
            for m in range(6):
                near = pltpu.roll(near_face, (128 - slot(m, c)) % 128, 1)
                nears[c].append(near)
                e = g[phase, m, c + 2, 8:16, :] * tile_sign[m]
                wall = pltpu.roll(e, c + 1, 1)
                pack_l[m] = jnp.where(lane == c, pltpu.roll(lr[m, c], c + 1, 1), pack_l[m])
                after = jnp.where(ri == 0, pltpu.roll(near, c, 1) if c else near, wall)
                pack_r[m] = jnp.where(lane == c, after, pack_r[m])
        extra = roe(pack_l, pack_r, 2)

        fc = roe([lc[m, 1] for m in range(6)], [rc[m, 2] for m in range(6)], 0)
        for c in range(4):
            fc_next = roe([lc[m, c + 2] for m in range(6)], [rc[m, c + 3] for m in range(6)], 0)
            e = [g[phase, m, c + 2, 8:16, :] for m in range(6)]
            left = [
                jnp.where(
                    hub_lane, e[m] * tile_sign[m], pltpu.roll(jnp.where(at_last, nears[c][m], lr[m, c]), 1, 1)
                )
                for m in range(6)
            ]
            fr = roe(left, [rr[m, c] for m in range(6)], 2)
            u0 = conserved(e)
            u1 = []
            for m in range(6):
                after = jnp.where(at_last, pltpu.roll(extra[m], 127 - c, 1), pltpu.roll(fr[m], 127, 1))
                total = (
                    (fc_next[m] - fc[m])
                    + (fa[m, c + 2, 9:17, :] - fa[m, c + 2, 8:16, :])
                    + (after - fr[m])
                )
                change = (-0.5 * STEP_SIZE) * total
                if m == 5:
                    change = change + STEP_SIZE * src[c]
                u1.append(u0[m] + change)
                out[m, c] = jnp.where(phase == 0, u0[m], out[m, c]) + 0.5 * change
            w = primitive(u1)
            for m in range(6):
                g[phase + 1, m, c + 2, 8:16, :] = w[m]
            fc = fc_next
        fill(phase + 1)
        return carry

    load.wait()
    kind.wait()
    for part in enter:
        part.wait()
    station_signs()
    pl.when(first)(entry_rows)
    fill(0)
    pl.semaphore_wait(barrier, FAR + BESIDE - 4 * first.astype(jnp.int32) - 4 * last.astype(jnp.int32))
    lax.fori_loop(0, 2, section, 0)
    for phase in range(2):
        each(MESSAGES, lambda k: far(phase, k).wait_send(), False, (True, False))
        each(PACKED, lambda k: beside(phase, k).wait_send(), False, (True, False))


def solution(mesh):
    def vmem(*shape):
        return pltpu.VMEM(shape, jnp.float32)

    def body(flow, inflow, wall_kind):
        padded = (6, PLANES, ROWS, 128)
        tiles = (6, PLANES, 8, 128)
        inner = (6, 4, 8, 128)
        return pl.pallas_call(
            kernel,
            out_shape=pltpu.VMEM(flow.shape, jnp.float32),
            in_specs=[pl.BlockSpec(memory_space=pl.ANY)] * 3,
            out_specs=pl.BlockSpec(memory_space=pltpu.VMEM),
            scratch_shapes=[
                vmem(3, *padded), vmem(3, 24, 128), vmem(2, BESIDE, 24, 128), vmem(24, 128),
                vmem(*tiles), vmem(*tiles), vmem(*tiles), vmem(*padded), vmem(*padded), vmem(*inner), vmem(*inner),
                vmem(4, 8, 128), vmem(*padded), vmem(ROWS, 128), vmem(2, 6, inflow.shape[1], 128), vmem(8, 128),
                pltpu.SMEM((2, wall_kind.shape[0]), jnp.int32),
                pltpu.SemaphoreType.DMA((4,)),
                pltpu.SemaphoreType.DMA((2, FAR + BESIDE)), pltpu.SemaphoreType.DMA((2, FAR + BESIDE)),
            ],
            compiler_params=pltpu.CompilerParams(
                collective_id=0, has_side_effects=True, vmem_limit_bytes=56 * 2**20
            ),
        )(flow, inflow, wall_kind.T)

    spec = P(None, "circ", "axial", "rad")
    return jax.shard_map(body, mesh=mesh, in_specs=(spec, P(), P()), out_specs=spec, check_vma=False)
```

```python
import jax
import jax.numpy as jnp
from jax import lax
from jax.experimental import pallas as pl
from jax.experimental.pallas import tpu as pltpu
from jax.sharding import PartitionSpec as P

MESH = pl.DeviceIdType.MESH
STEP_SIZE = 0.15
LIMIT_EPS = 0.03
FIX_WIDTH = 0.2
PRODUCE = 0.1355
DESTROY = 3.24

PLANES = 14
OWN = 5
ROWS = 24

MESSAGES = (
    (0, 1, (5, 9), (14, 16), (5, 9), (6, 8)),
    (0, -1, (5, 9), (8, 10), (5, 9), (16, 18)),
    (1, 1, (8, 9), (15, 16), (4, 5), (7, 8)),
    (1, -1, (8, 9), (8, 9), (4, 5), (16, 17)),
    (-1, 1, (5, 6), (15, 16), (9, 10), (7, 8)),
    (-1, -1, (5, 6), (8, 9), (9, 10), (16, 17)),
    (1, 0, (7, 9), (8, 16), (3, 5), (8, 16)),
    (-1, 0, (5, 7), (8, 16), (9, 11), (8, 16)),
)
PACKED = (
    (0, 1, (0, 16)),
    (0, -1, (8, 24)),
    (1, 0, (8, 16)),
    (-1, 0, (8, 16)),
)
FAR, BESIDE = len(MESSAGES), len(PACKED)


def slot(m, c):
    return 2 * (m * 6 + 1 + c)


def across(ref, phase, m, row, first=OWN, count=8):
    return ref.at[pl.ds(((phase * 6 + m) * PLANES + first) * ROWS + row, count, stride=ROWS), :]


def flat(ref):
    return ref.reshape(ref.size // 128, 128)


def conserved(p):
    q = 0.5 * (p[1] * p[1] + p[2] * p[2] + p[3] * p[3])
    return [p[0], p[0] * p[1], p[0] * p[2], p[0] * p[3], 2.5 * p[4] + p[0] * q, p[0] * p[5]]


def primitive(u):
    inv = 1.0 / u[0]
    v = [u[1] * inv, u[2] * inv, u[3] * inv]
    pressure = 0.4 * (u[4] - 0.5 * u[0] * (v[0] * v[0] + v[1] * v[1] + v[2] * v[2]))
    return [u[0], v[0], v[1], v[2], pressure, u[5] * inv]


def reach(*tiles):
    top = low = tiles[0]
    for t in tiles[1:]:
        top, low = jnp.maximum(top, t), jnp.minimum(low, t)
    return top, low


def limit(e, top, low, dc, ap, am, dr):
    da = ap - am
    top, low = jnp.maximum(top, jnp.maximum(ap, am)), jnp.minimum(low, jnp.minimum(ap, am))
    bound = jnp.minimum(top - e, e - low)
    delta = 0.25 * jnp.maximum(jnp.maximum(jnp.abs(dc), jnp.abs(da)), jnp.abs(dr))
    square = bound * bound + LIMIT_EPS
    cross = bound * delta
    factor = jnp.minimum(1.0, (square + 2.0 * cross) / (square + cross + 2.0 * delta * delta))
    quarter = 0.25 * factor
    return (quarter * dc, quarter * da, quarter * dr), (dc, da, dr)


def limit_all(e, cp, cm, ap, am, rp, rm):
    return limit(e, *reach(e, cp, cm, rp, rm), cp - cm, ap, am, rp - rm)


def fix(speed):
    size = jnp.abs(speed)
    return jnp.where(size < FIX_WIDTH, speed * speed * (0.5 / FIX_WIDTH) + 0.5 * FIX_WIDTH, size)


def side(s, d):
    y = lax.rsqrt(s[0])
    root = s[0] * y
    q = 0.5 * (s[1] * s[1] + s[2] * s[2] + s[3] * s[3])
    h = 3.5 * s[4] * (y * y) + q
    m = s[0] * s[d + 1]
    f = [m, m * s[1], m * s[2], m * s[3], m * h, m * s[5]]
    f[d + 1] = f[d + 1] + s[4]
    return root, h, f


def roe(left, right, d):
    rl, hl, fl = side(left, d)
    rr, hr, fr = side(right, d)
    jump = [r - l for l, r in zip(left, right)]
    w = rr / (rl + rr)
    vel = [left[k] + w * jump[k] for k in (1, 2, 3)]
    h = hl + w * (hr - hl)
    nu = left[5] + w * jump[5]
    un = vel[d]
    q = 0.5 * (vel[0] * vel[0] + vel[1] * vel[1] + vel[2] * vel[2])
    c2 = 0.4 * (h - q)
    ic = lax.rsqrt(c2)
    c = c2 * ic
    dens = rl * rr
    x = 0.5 * jump[4] * (ic * ic)
    y = 0.5 * dens * jump[d + 1] * ic
    mid = fix(un)
    slow = fix(un - c) * (x - y)
    fast = fix(un + c) * (x + y)
    both = slow + fast
    wave = mid * (jump[0] - 2.0 * x)
    total = both + wave
    skew = c * (fast - slow)
    shear = mid * dens
    dis = [total]
    inner = None
    for k in range(3):
        if k == d:
            dis.append(total * vel[k] + skew)
        else:
            part = shear * jump[k + 1]
            dis.append(total * vel[k] + part)
            inner = vel[k] * part if inner is None else inner + vel[k] * part
    dis.append(both * h + un * skew + wave * q + inner)
    dis.append(total * nu + shear * jump[5])
    return [fl[k] + fr[k] - dis[k] for k in range(6)]


def kernel(
    flow, inflow, walls, out,
    g, pack, land, packed, top, low, slant, lc, rc, ap, am, rin, rout, src, fa, ns, entry, entry_packed, kinds,
    local_sem, send_sem, recv_sem,
):
    ci, ai, ri = lax.axis_index("circ"), lax.axis_index("axial"), lax.axis_index("rad")
    nc, na = lax.axis_size("circ"), lax.axis_size("axial")
    first, last = ai == 0, ai == na - 1

    def target(dc, da, cross=False):
        return {"circ": lax.rem(ci + dc + nc, nc), "axial": ai + da, "rad": 1 - ri if cross else ri}

    twin = {"circ": ci, "axial": ai, "rad": 1 - ri}

    def guard(da, act):
        if da == 0:
            act()
        else:
            pl.when(ai < na - 1 if da > 0 else ai > 0)(act)

    barrier = pltpu.get_barrier_semaphore()
    for cross, group in ((False, MESSAGES), (True, PACKED)):
        for dc, da, *_ in group:
            guard(da, lambda dc=dc, da=da, cross=cross: pl.semaphore_signal(
                barrier, inc=1, device_id=target(dc, da, cross), device_id_type=MESH))
    pl.semaphore_signal(barrier, inc=1, device_id=twin, device_id_type=MESH)

    load = pltpu.make_async_copy(flow, g.at[0, :, OWN:OWN + 4, 8:16, :], local_sem.at[0])
    load.start()
    kind = pltpu.make_async_copy(walls, kinds, local_sem.at[1])
    kind.start()
    enter = [
        pltpu.make_async_copy(
            inflow.at[:, :, pl.ds(pl.multiple_of(core * 128, 128), 128)], entry.at[k], local_sem.at[2 + k])
        for k, core in enumerate((ri, 1 - ri))
    ]
    for part in enter:
        part.start()

    def remote(phase, k, source, into, device):
        return pltpu.make_async_remote_copy(
            src_ref=source, dst_ref=into, send_sem=send_sem.at[phase, k], recv_sem=recv_sem.at[phase, k],
            device_id=device, device_id_type=MESH,
        )

    def far(phase, k):
        dc, da, sp, sr, tp, tr = MESSAGES[k]
        return remote(
            phase, k, g.at[phase, :, sp[0]:sp[1], sr[0]:sr[1], :], g.at[phase, :, tp[0]:tp[1], tr[0]:tr[1], :],
            target(dc, da))

    def direct(phase, k):
        dc, da, (low, high) = PACKED[k]
        return remote(
            phase, FAR + k, pack.at[phase, low:high, :], land.at[phase, k, low:high, :], target(dc, da, True))

    def own_column(phase):
        return remote(phase, FAR + BESIDE, pack.at[phase, 8:16, :], land.at[phase, BESIDE, 8:16, :], twin)

    def each(group, act, back, along_axis):
        for k, (dc, da, *_) in enumerate(group):
            if (da != 0) == along_axis:
                guard(-da if back else da, lambda k=k: act(k))

    lane = lax.broadcasted_iota(jnp.int32, (8, 128), 1)
    low_rows = lax.broadcasted_iota(jnp.int32, (8, 128), 0) < 4
    at_wall, at_edge = lane == 127 * ri, lane == 127 * (1 - ri)
    inward, outward = jnp.where(ri == 0, 127, 1), jnp.where(ri == 0, 1, 127)
    facing = jnp.where(ri == 0, 1.0, -1.0)
    radial = ri * 128 + lane
    wall_inv = 1.0 / (jnp.minimum(radial, 255 - radial) + 1).astype(jnp.float32)

    def around(e, near, sign):
        inner = pltpu.roll(jnp.where(at_wall, near, e), inward, 1)
        return inner, jnp.where(at_wall, e * sign, pltpu.roll(e, outward, 1))

    def signs(tile):
        return (1.0, tile, tile, -1.0, 1.0, tile)

    def fill(phase):
        tile = jnp.zeros((8, 128), jnp.float32)
        for m in range(6):
            for c in range(4):
                at = slot(m, c)
                e = g[phase, m, OWN + c, 8:16, :]
                turned = pltpu.roll(e, jnp.where(ri == 0, (at + 2) % 128, at), 1)
                tile = jnp.where((lane == at) | (lane == at + 1), turned, tile)
        pack[phase, 8:16, :] = tile
        for row, start in ((15, 0), (8, 20)):
            tile = jnp.zeros((4, 128), jnp.float32)
            for m in range(6):
                e = across(flat(g), phase, m, row, OWN, 4)[...]
                here = lane[0:4] == lax.rem(m + 127 * (1 - ri), 128)
                tile = jnp.where(here, pltpu.roll(e, m, 1) if m else e, tile)
            pack[phase, start:start + 4, :] = tile

    def station_signs():
        for row in range(7, 17):
            station = jnp.clip(ai * 8 + (row - 8), 0, na * 8 - 1)
            value = jnp.where(kinds[ri, station] == 1, -1.0, 1.0)
            ns[pl.ds(row, 1), :] = jnp.full((1, 128), value, jnp.float32)

    def entry_rows():
        row = jnp.zeros((1, 128), jnp.float32)
        for m in range(6):
            for c in range(-1, 5):
                at = lax.rem(ci * 4 + c + nc * 4, nc * 4)
                mine = entry[0, m, pl.ds(at, 1), :]
                for phase in range(2):
                    g[phase, m, OWN + c, 7:8, :] = mine
                if 0 <= c < 4:
                    theirs = entry[1, m, pl.ds(at, 1), :]
                    k = slot(m, c)
                    turned = pltpu.roll(
                        jnp.broadcast_to(theirs, (8, 128)), jnp.where(ri == 0, k, (k + 2) % 128), 1)[0:1]
                    row = jnp.where((lane[0:1] == k) | (lane[0:1] == k + 1), turned, row)
        entry_packed[0:1, :] = row

    def section(phase, carry):
        each(MESSAGES, lambda k: far(phase, k).start(), False, True)
        each(PACKED, lambda k: direct(phase, k).start(), False, True)
        own_column(phase).start()
        each(PACKED, lambda k: direct(phase, k).start(), False, False)
        each(MESSAGES, lambda k: far(phase, k).start(), False, False)

        def cell(m, c):
            return g[phase, m, OWN + c, 8:16, :]

        def turned(tile):
            return pltpu.roll(tile, jnp.where(ri == 0, 0, 126), 1)

        tile_sign = signs(ns[8:16, :])

        def prepare(c, columns, shift):
            for m in range(6):
                e = cell(m, c)
                inner, outer = around(e, pltpu.roll(columns, (128 - slot(m, shift)) % 128, 1), tile_sign[m])
                top[m, c + 1], low[m, c + 1] = reach(e, cell(m, c + 1), cell(m, c - 1), inner, outer)
                slant[m, c + 1] = inner - outer

        own_column(phase).wait_recv()
        each(MESSAGES, lambda k: far(phase, k).wait_recv(), True, False)
        ours = turned(land[phase, BESIDE, 8:16, :])
        for c in range(4):
            prepare(c, ours, c)
        each(PACKED, lambda k: direct(phase, k).wait_recv(), True, False)
        prepare(-1, turned(land[phase, 2, 8:16, :]), 3)
        prepare(4, turned(land[phase, 3, 8:16, :]), 0)

        each(MESSAGES, lambda k: far(phase, k).wait_recv(), True, True)

        @pl.when(last)
        def _():
            for m in range(6):
                for plane in range(OWN - 1, OWN + 5):
                    g[phase, m, plane, 16:17, :] = g[phase, m, plane, 15:16, :]

        def slopes(m, c):
            e = cell(m, c)
            return e, *limit(
                e, top[m, c + 1], low[m, c + 1], cell(m, c + 1) - cell(m, c - 1),
                g[phase, m, OWN + c, 9:17, :], g[phase, m, OWN + c, 7:15, :], slant[m, c + 1])

        def circ_face(c):
            return roe([lc[m, c] for m in range(6)], [rc[m, c + 1] for m in range(6)], 0)

        for c in range(4):
            diffs = []
            for m in range(6):
                e, hs, diff = slopes(m, c)
                diffs.append(diff)
                lc[m, c + 1] = e + hs[0]
                rc[m, c + 1] = e - hs[0]
                ap[m, OWN + c, 8:16, :] = e + hs[1]
                am[m, OWN + c, 8:16, :] = e - hs[1]
                scale = facing if m == 3 else 1.0
                rin[m, c] = (e + hs[2]) * scale
                rout[m, c] = (e - hs[2]) * scale
            oc = diffs[3][1] - diffs[2][2] * facing
            oa = diffs[1][2] * facing - diffs[3][0]
            orr = diffs[2][0] - diffs[1][1]
            s = jnp.sqrt(oc * oc + oa * oa + orr * orr)
            dens, nu = cell(0, c), cell(5, c)
            ratio = nu * wall_inv
            src[c] = (0.5 * PRODUCE) * s * dens * nu - DESTROY * dens * (ratio * ratio)

        radial_faces = []
        for c in range(4):
            ghost = [cell(m, c) * tile_sign[m] for m in range(6)]
            ghost[3] = ghost[3] * facing
            left = [jnp.where(at_wall, ghost[m], pltpu.roll(rin[m, c], outward, 1)) for m in range(6)]
            radial_faces.append(roe(left, [rout[m, c] for m in range(6)], 2))
        circ_faces = [None] + [circ_face(c) for c in range(1, 4)] + [None]


        for m in range(6):
            e, hs, _ = slopes(m, -1)
            lc[m, 0] = e + hs[0]
            e, hs, _ = slopes(m, 4)
            rc[m, 5] = e - hs[0]
        circ_faces[0], circ_faces[4] = circ_face(0), circ_face(4)

        each(PACKED, lambda k: direct(phase, k).wait_recv(), True, True)

        g_f, ap_f, am_f, fa_f = flat(g), flat(ap), flat(am), flat(fa)

        def both(m, step_row, step_plane):
            return jnp.where(
                low_rows,
                across(g_f, phase, m, 7 + step_row, OWN + step_plane)[...],
                across(g_f, phase, m, 16 + step_row, OWN - 4 + step_plane)[...])

        row_sign = signs(jnp.where(
            low_rows, jnp.broadcast_to(ns[7:8, :], (8, 128)), jnp.broadcast_to(ns[16:17, :], (8, 128))))
        columns = jnp.where(low_rows, land[phase, 0, 0:8, :], land[phase, 1, 16:24, :])
        outside = (low_rows & first) | (jnp.logical_not(low_rows) & last)
        for m in range(6):
            e = both(m, 0, 0)
            inner, outer = around(e, pltpu.roll(columns, 128 - m, 1) if m else columns, row_sign[m])
            hs, _ = limit_all(e, both(m, 0, 1), both(m, 0, -1), both(m, 1, 0), both(m, -1, 0), inner, outer)
            slope = jnp.where(outside, 0.0, hs[1])
            across(ap_f, 0, m, 7, OWN)[...] = e + slope
            across(am_f, 0, m, 16, OWN - 4)[...] = e - slope

        place = lax.rem(lane // 2, 6)
        halo = jnp.where(place == 0, pltpu.roll(land[phase, 2, 8:16, :], 120, 1), land[phase, BESIDE, 8:16, :])
        halo = jnp.where(place == 5, pltpu.roll(land[phase, 3, 8:16, :], 8, 1), halo)
        packed[8:16, :] = halo
        packed[7:8, :] = jnp.where(first, entry_packed[0:1, :], land[phase, 0, 15:16, :])
        packed[16:17, :] = jnp.where(last, packed[15:16, :], land[phase, 1, 8:9, :])
        beyond, mine = pltpu.roll(halo, inward, 1), pltpu.roll(pack[phase, 8:16, :], inward, 1)
        hs, _ = limit_all(
            halo, pltpu.roll(halo, 126, 1), pltpu.roll(halo, 2, 1), packed[9:17, :], packed[7:15, :], beyond, mine
        )
        near_face = halo - hs[2]

        left, right = [], []
        for m in range(6):
            tile = rin[m, 0]
            for c in range(1, 4):
                tile = jnp.where(at_edge, rin[m, c], pltpu.roll(tile, 126, 1))
            left.append(tile)
            right.append(pltpu.roll(near_face, (121 - slot(m, 0)) % 128, 1))
        right[3] = right[3] * facing
        middle = roe(left, right, 2)

        for c in range(4):
            f = roe([ap[m, OWN + c, 7:15, :] for m in range(6)], [am[m, OWN + c, 8:16, :] for m in range(6)], 1)
            for m in range(6):
                fa[m, OWN + c, 8:16, :] = f[m]
        f = roe([across(ap_f, 0, m, 15)[...] for m in range(6)], [across(am_f, 0, m, 16)[...] for m in range(6)], 1)
        for m in range(6):
            across(fa_f, 0, m, 16)[...] = f[m]
        for c in range(4):
            u0 = conserved([cell(m, c) for m in range(6)])
            u1 = []
            for m in range(6):
                face = radial_faces[c][m]
                inner = jnp.where(
                    at_edge, pltpu.roll(middle[m], 6 - 2 * c, 1) if c < 3 else middle[m], pltpu.roll(face, inward, 1))
                along = inner - face
                if m == 3:
                    along = along * facing
                total = (
                    (circ_faces[c + 1][m] - circ_faces[c][m])
                    + (fa[m, OWN + c, 9:17, :] - fa[m, OWN + c, 8:16, :])
                    + along
                )
                change = (-0.5 * STEP_SIZE) * total
                if m == 5:
                    change = change + STEP_SIZE * src[c]
                u1.append(u0[m] + change)
                out[m, c] = jnp.where(phase == 0, u0[m], out[m, c]) + 0.5 * change
            w = primitive(u1)
            for m in range(6):
                g[phase + 1, m, OWN + c, 8:16, :] = w[m]
        fill(phase + 1)
        return carry

    load.wait()
    kind.wait()
    for part in enter:
        part.wait()
    station_signs()
    pl.when(first)(entry_rows)
    fill(0)
    pl.semaphore_wait(barrier, FAR + BESIDE + 1 - 4 * first.astype(jnp.int32) - 4 * last.astype(jnp.int32))
    lax.fori_loop(0, 2, section, 0)
    for phase in range(2):
        own_column(phase).wait_send()
        for along_axis in (True, False):
            each(MESSAGES, lambda k: far(phase, k).wait_send(), False, along_axis)
            each(PACKED, lambda k: direct(phase, k).wait_send(), False, along_axis)


def solution(mesh):
    def vmem(*shape):
        return pltpu.VMEM(shape, jnp.float32)

    def body(flow, inflow, wall_kind):
        padded = (6, PLANES, ROWS, 128)
        tiles = (6, 6, 8, 128)
        inner = (6, 4, 8, 128)
        copies = FAR + BESIDE + 1
        return pl.pallas_call(
            kernel,
            out_shape=pltpu.VMEM(flow.shape, jnp.float32),
            in_specs=[pl.BlockSpec(memory_space=pl.ANY)] * 3,
            out_specs=pl.BlockSpec(memory_space=pltpu.VMEM),
            scratch_shapes=[
                vmem(3, *padded), vmem(3, 24, 128), vmem(2, BESIDE + 1, 24, 128),
                vmem(24, 128), vmem(*tiles), vmem(*tiles), vmem(*tiles), vmem(*tiles), vmem(*tiles), vmem(*padded), vmem(*padded), vmem(*inner), vmem(*inner),
                vmem(4, 8, 128), vmem(*padded), vmem(ROWS, 128), vmem(2, 6, inflow.shape[1], 128), vmem(8, 128),
                pltpu.SMEM((2, wall_kind.shape[0]), jnp.int32),
                pltpu.SemaphoreType.DMA((4,)),
                pltpu.SemaphoreType.DMA((2, copies)), pltpu.SemaphoreType.DMA((2, copies)),
            ],
            compiler_params=pltpu.CompilerParams(
                collective_id=0, has_side_effects=True, vmem_limit_bytes=56 * 2**20
            ),
        )(flow, inflow, wall_kind.T)

    spec = P(None, "circ", "axial", "rad")
    return jax.shard_map(body, mesh=mesh, in_specs=(spec, P(), P()), out_specs=spec, check_vma=False)
```

```python
import jax
import jax.numpy as jnp
from jax import lax
from jax.experimental import pallas as pl
from jax.experimental.pallas import tpu as pltpu
from jax.sharding import PartitionSpec as P

MESH = pl.DeviceIdType.MESH
STEP_SIZE = 0.15
LIMIT_EPS = 0.03
FIX_WIDTH = 0.2
PRODUCE = 0.1355
DESTROY = 3.24

PLANES = 14
OWN = 5
ROWS = 24

MESSAGES = (
    (0, 1, (5, 9), (14, 16), (5, 9), (6, 8)),
    (0, -1, (5, 9), (8, 10), (5, 9), (16, 18)),
    (1, 1, (8, 9), (15, 16), (4, 5), (7, 8)),
    (1, -1, (8, 9), (8, 9), (4, 5), (16, 17)),
    (-1, 1, (5, 6), (15, 16), (9, 10), (7, 8)),
    (-1, -1, (5, 6), (8, 9), (9, 10), (16, 17)),
    (1, 0, (7, 9), (8, 16), (3, 5), (8, 16)),
    (-1, 0, (5, 7), (8, 16), (9, 11), (8, 16)),
)
PACKED = (
    (0, 1, (0, 16)),
    (0, -1, (8, 24)),
    (1, 0, (8, 16)),
    (-1, 0, (8, 16)),
)
FAR, BESIDE = len(MESSAGES), len(PACKED)


def slot(m, c):
    return 2 * (m * 6 + 1 + c)


def across(ref, phase, m, row, first=OWN, count=8):
    return ref.at[pl.ds(((phase * 6 + m) * PLANES + first) * ROWS + row, count, stride=ROWS), :]


def flat(ref):
    return ref.reshape(ref.size // 128, 128)


def conserved(p):
    q = 0.5 * (p[1] * p[1] + p[2] * p[2] + p[3] * p[3])
    return [p[0], p[0] * p[1], p[0] * p[2], p[0] * p[3], 2.5 * p[4] + p[0] * q, p[0] * p[5]]


def primitive(u):
    inv = 1.0 / u[0]
    v = [u[1] * inv, u[2] * inv, u[3] * inv]
    pressure = 0.4 * (u[4] - 0.5 * u[0] * (v[0] * v[0] + v[1] * v[1] + v[2] * v[2]))
    return [u[0], v[0], v[1], v[2], pressure, u[5] * inv]


def reach(*tiles):
    top = low = tiles[0]
    for t in tiles[1:]:
        top, low = jnp.maximum(top, t), jnp.minimum(low, t)
    return top, low


def limit(e, top, low, dc, ap, am, dr):
    da = ap - am
    top, low = jnp.maximum(top, jnp.maximum(ap, am)), jnp.minimum(low, jnp.minimum(ap, am))
    bound = jnp.minimum(top - e, e - low)
    delta = 0.25 * jnp.maximum(jnp.maximum(jnp.abs(dc), jnp.abs(da)), jnp.abs(dr))
    square = bound * bound + LIMIT_EPS
    cross = bound * delta
    factor = jnp.minimum(1.0, (square + 2.0 * cross) / (square + cross + 2.0 * delta * delta))
    quarter = 0.25 * factor
    return (quarter * dc, quarter * da, quarter * dr), (dc, da, dr)


def limit_all(e, cp, cm, ap, am, rp, rm):
    return limit(e, *reach(e, cp, cm, rp, rm), cp - cm, ap, am, rp - rm)


def fix(speed):
    size = jnp.abs(speed)
    return jnp.where(size < FIX_WIDTH, speed * speed * (0.5 / FIX_WIDTH) + 0.5 * FIX_WIDTH, size)


def side(s, d):
    y = lax.rsqrt(s[0])
    root = s[0] * y
    q = 0.5 * (s[1] * s[1] + s[2] * s[2] + s[3] * s[3])
    h = 3.5 * s[4] * (y * y) + q
    m = s[0] * s[d + 1]
    f = [m, m * s[1], m * s[2], m * s[3], m * h, m * s[5]]
    f[d + 1] = f[d + 1] + s[4]
    return root, h, f


def roe(left, right, d):
    rl, hl, fl = side(left, d)
    rr, hr, fr = side(right, d)
    jump = [r - l for l, r in zip(left, right)]
    w = rr / (rl + rr)
    vel = [left[k] + w * jump[k] for k in (1, 2, 3)]
    h = hl + w * (hr - hl)
    nu = left[5] + w * jump[5]
    un = vel[d]
    q = 0.5 * (vel[0] * vel[0] + vel[1] * vel[1] + vel[2] * vel[2])
    c2 = 0.4 * (h - q)
    ic = lax.rsqrt(c2)
    c = c2 * ic
    dens = rl * rr
    x = 0.5 * jump[4] * (ic * ic)
    y = 0.5 * dens * jump[d + 1] * ic
    mid = fix(un)
    slow = fix(un - c) * (x - y)
    fast = fix(un + c) * (x + y)
    both = slow + fast
    wave = mid * (jump[0] - 2.0 * x)
    total = both + wave
    skew = c * (fast - slow)
    shear = mid * dens
    dis = [total]
    inner = None
    for k in range(3):
        if k == d:
            dis.append(total * vel[k] + skew)
        else:
            part = shear * jump[k + 1]
            dis.append(total * vel[k] + part)
            inner = vel[k] * part if inner is None else inner + vel[k] * part
    dis.append(both * h + un * skew + wave * q + inner)
    dis.append(total * nu + shear * jump[5])
    return [fl[k] + fr[k] - dis[k] for k in range(6)]


def kernel(
    flow, inflow, walls, out,
    g, pack, land, packed, top, low, slant, lc, rc, ap, am, rin, rout, src, fa, ns, entry, entry_packed, kinds,
    local_sem, send_sem, recv_sem,
):
    ci, ai, ri = lax.axis_index("circ"), lax.axis_index("axial"), lax.axis_index("rad")
    nc, na = lax.axis_size("circ"), lax.axis_size("axial")
    first, last = ai == 0, ai == na - 1

    def target(dc, da, cross=False):
        return {"circ": lax.rem(ci + dc + nc, nc), "axial": ai + da, "rad": 1 - ri if cross else ri}

    twin = {"circ": ci, "axial": ai, "rad": 1 - ri}

    def guard(da, act):
        if da == 0:
            act()
        else:
            pl.when(ai < na - 1 if da > 0 else ai > 0)(act)

    barrier = pltpu.get_barrier_semaphore()
    for cross, group in ((False, MESSAGES), (True, PACKED)):
        for dc, da, *_ in group:
            guard(da, lambda dc=dc, da=da, cross=cross: pl.semaphore_signal(
                barrier, inc=1, device_id=target(dc, da, cross), device_id_type=MESH))
    pl.semaphore_signal(barrier, inc=1, device_id=twin, device_id_type=MESH)

    load = pltpu.make_async_copy(flow, g.at[0, :, OWN:OWN + 4, 8:16, :], local_sem.at[0])
    load.start()
    kind = pltpu.make_async_copy(walls, kinds, local_sem.at[1])
    kind.start()
    enter = [
        pltpu.make_async_copy(
            inflow.at[:, :, pl.ds(pl.multiple_of(core * 128, 128), 128)], entry.at[k], local_sem.at[2 + k])
        for k, core in enumerate((ri, 1 - ri))
    ]
    for part in enter:
        part.start()

    def remote(phase, k, source, into, device):
        return pltpu.make_async_remote_copy(
            src_ref=source, dst_ref=into, send_sem=send_sem.at[phase, k], recv_sem=recv_sem.at[phase, k],
            device_id=device, device_id_type=MESH,
        )

    def far(phase, k):
        dc, da, sp, sr, tp, tr = MESSAGES[k]
        return remote(
            phase, k, g.at[phase, :, sp[0]:sp[1], sr[0]:sr[1], :], g.at[phase, :, tp[0]:tp[1], tr[0]:tr[1], :],
            target(dc, da))

    def direct(phase, k):
        dc, da, (low, high) = PACKED[k]
        return remote(
            phase, FAR + k, pack.at[phase, low:high, :], land.at[phase, k, low:high, :], target(dc, da, True))

    def own_column(phase):
        return remote(phase, FAR + BESIDE, pack.at[phase, 8:16, :], land.at[phase, BESIDE, 8:16, :], twin)

    def each(group, act, back, along_axis):
        for k, (dc, da, *_) in enumerate(group):
            if (da != 0) == along_axis:
                guard(-da if back else da, lambda k=k: act(k))

    lane = lax.broadcasted_iota(jnp.int32, (8, 128), 1)
    low_rows = lax.broadcasted_iota(jnp.int32, (8, 128), 0) < 4
    at_wall, at_edge = lane == 127 * ri, lane == 127 * (1 - ri)
    inward, outward = jnp.where(ri == 0, 127, 1), jnp.where(ri == 0, 1, 127)
    facing = jnp.where(ri == 0, 1.0, -1.0)
    radial = ri * 128 + lane
    wall_inv = 1.0 / (jnp.minimum(radial, 255 - radial) + 1).astype(jnp.float32)

    def around(e, near, sign):
        inner = pltpu.roll(jnp.where(at_wall, near, e), inward, 1)
        return inner, jnp.where(at_wall, e * sign, pltpu.roll(e, outward, 1))

    def signs(tile):
        return (1.0, tile, tile, -1.0, 1.0, tile)

    def fill(phase):
        tile = jnp.zeros((8, 128), jnp.float32)
        for m in range(6):
            for c in range(4):
                at = slot(m, c)
                e = g[phase, m, OWN + c, 8:16, :]
                turned = pltpu.roll(e, jnp.where(ri == 0, (at + 2) % 128, at), 1)
                tile = jnp.where((lane == at) | (lane == at + 1), turned, tile)
        pack[phase, 8:16, :] = tile
        for row, start in ((15, 0), (8, 20)):
            tile = jnp.zeros((4, 128), jnp.float32)
            for m in range(6):
                e = across(flat(g), phase, m, row, OWN, 4)[...]
                here = lane[0:4] == lax.rem(m + 127 * (1 - ri), 128)
                tile = jnp.where(here, pltpu.roll(e, m, 1) if m else e, tile)
            pack[phase, start:start + 4, :] = tile

    def station_signs():
        for row in range(7, 17):
            station = jnp.clip(ai * 8 + (row - 8), 0, na * 8 - 1)
            value = jnp.where(kinds[ri, station] == 1, -1.0, 1.0)
            ns[pl.ds(row, 1), :] = jnp.full((1, 128), value, jnp.float32)

    def entry_rows():
        row = jnp.zeros((1, 128), jnp.float32)
        for m in range(6):
            for c in range(-1, 5):
                at = lax.rem(ci * 4 + c + nc * 4, nc * 4)
                mine = entry[0, m, pl.ds(at, 1), :]
                for phase in range(2):
                    g[phase, m, OWN + c, 7:8, :] = mine
                if 0 <= c < 4:
                    theirs = entry[1, m, pl.ds(at, 1), :]
                    k = slot(m, c)
                    turned = pltpu.roll(
                        jnp.broadcast_to(theirs, (8, 128)), jnp.where(ri == 0, k, (k + 2) % 128), 1)[0:1]
                    row = jnp.where((lane[0:1] == k) | (lane[0:1] == k + 1), turned, row)
        entry_packed[0:1, :] = row

    def section(phase, carry):
        each(MESSAGES, lambda k: far(phase, k).start(), False, True)

        @pl.when(phase > 0)
        def _():
            fill(phase)

        own_column(phase).start()
        each(PACKED, lambda k: direct(phase, k).start(), False, True)
        each(PACKED, lambda k: direct(phase, k).start(), False, False)
        each(MESSAGES, lambda k: far(phase, k).start(), False, False)

        @pl.when(phase == 0)
        def _():
            kind.wait()
            for part in enter:
                part.wait()
            station_signs()
            pl.when(first)(entry_rows)

        def cell(m, c):
            return g[phase, m, OWN + c, 8:16, :]

        def turned(tile):
            return pltpu.roll(tile, jnp.where(ri == 0, 0, 126), 1)

        tile_sign = signs(ns[8:16, :])

        def prepare(c, columns, shift):
            for m in range(6):
                e = cell(m, c)
                inner, outer = around(e, pltpu.roll(columns, (128 - slot(m, shift)) % 128, 1), tile_sign[m])
                top[m, c + 1], low[m, c + 1] = reach(e, cell(m, c + 1), cell(m, c - 1), inner, outer)
                slant[m, c + 1] = inner - outer

        own_column(phase).wait_recv()
        each(MESSAGES, lambda k: far(phase, k).wait_recv(), True, False)
        ours = turned(land[phase, BESIDE, 8:16, :])
        for c in range(4):
            prepare(c, ours, c)

        each(MESSAGES, lambda k: far(phase, k).wait_recv(), True, True)

        @pl.when(last)
        def _():
            for m in range(6):
                for plane in range(OWN - 1, OWN + 5):
                    g[phase, m, plane, 16:17, :] = g[phase, m, plane, 15:16, :]

        def slopes(m, c):
            e = cell(m, c)
            return e, *limit(
                e, top[m, c + 1], low[m, c + 1], cell(m, c + 1) - cell(m, c - 1),
                g[phase, m, OWN + c, 9:17, :], g[phase, m, OWN + c, 7:15, :], slant[m, c + 1])

        def circ_face(c):
            return roe([lc[m, c] for m in range(6)], [rc[m, c + 1] for m in range(6)], 0)

        for c in range(4):
            diffs = []
            for m in range(6):
                e, hs, diff = slopes(m, c)
                diffs.append(diff)
                lc[m, c + 1] = e + hs[0]
                rc[m, c + 1] = e - hs[0]
                ap[m, OWN + c, 8:16, :] = e + hs[1]
                am[m, OWN + c, 8:16, :] = e - hs[1]
                scale = facing if m == 3 else 1.0
                rin[m, c] = (e + hs[2]) * scale
                rout[m, c] = (e - hs[2]) * scale
            oc = diffs[3][1] - diffs[2][2] * facing
            oa = diffs[1][2] * facing - diffs[3][0]
            orr = diffs[2][0] - diffs[1][1]
            s = jnp.sqrt(oc * oc + oa * oa + orr * orr)
            dens, nu = cell(0, c), cell(5, c)
            ratio = nu * wall_inv
            src[c] = (0.5 * PRODUCE) * s * dens * nu - DESTROY * dens * (ratio * ratio)

        radial_faces = []
        for c in range(4):
            ghost = [cell(m, c) * tile_sign[m] for m in range(6)]
            ghost[3] = ghost[3] * facing
            left = [jnp.where(at_wall, ghost[m], pltpu.roll(rin[m, c], outward, 1)) for m in range(6)]
            radial_faces.append(roe(left, [rout[m, c] for m in range(6)], 2))
        circ_faces = [None] + [circ_face(c) for c in range(1, 4)] + [None]


        each(PACKED, lambda k: direct(phase, k).wait_recv(), True, False)
        prepare(-1, turned(land[phase, 2, 8:16, :]), 3)
        prepare(4, turned(land[phase, 3, 8:16, :]), 0)

        for m in range(6):
            e, hs, _ = slopes(m, -1)
            lc[m, 0] = e + hs[0]
            e, hs, _ = slopes(m, 4)
            rc[m, 5] = e - hs[0]
        circ_faces[0], circ_faces[4] = circ_face(0), circ_face(4)

        for c in range(4):
            f = roe([ap[m, OWN + c, 7:15, :] for m in range(6)], [am[m, OWN + c, 8:16, :] for m in range(6)], 1)
            for m in range(6):
                fa[m, OWN + c, 8:16, :] = f[m]

        before, starts, inners = [], [], []
        for c in range(4):
            starts.append(conserved([cell(m, c) for m in range(6)]))
            before.append([])
            inners.append([])
            for m in range(6):
                face = radial_faces[c][m] * facing if m == 3 else radial_faces[c][m]
                inners[c].append(pltpu.roll(face, inward, 1))
                before[c].append((circ_faces[c + 1][m] - circ_faces[c][m]) - face)
        left = []
        for m in range(6):
            tile = rin[m, 0]
            for c in range(1, 4):
                tile = jnp.where(at_edge, rin[m, c], pltpu.roll(tile, 126, 1))
            left.append(tile)

        each(PACKED, lambda k: direct(phase, k).wait_recv(), True, True)

        g_f, ap_f, am_f, fa_f = flat(g), flat(ap), flat(am), flat(fa)

        def both(m, step_row, step_plane):
            return jnp.where(
                low_rows,
                across(g_f, phase, m, 7 + step_row, OWN + step_plane)[...],
                across(g_f, phase, m, 16 + step_row, OWN - 4 + step_plane)[...])

        row_sign = signs(jnp.where(
            low_rows, jnp.broadcast_to(ns[7:8, :], (8, 128)), jnp.broadcast_to(ns[16:17, :], (8, 128))))
        columns = jnp.where(low_rows, land[phase, 0, 0:8, :], land[phase, 1, 16:24, :])
        outside = (low_rows & first) | (jnp.logical_not(low_rows) & last)
        for m in range(6):
            e = both(m, 0, 0)
            inner, outer = around(e, pltpu.roll(columns, 128 - m, 1) if m else columns, row_sign[m])
            hs, _ = limit_all(e, both(m, 0, 1), both(m, 0, -1), both(m, 1, 0), both(m, -1, 0), inner, outer)
            slope = jnp.where(outside, 0.0, hs[1])
            across(ap_f, 0, m, 7, OWN)[...] = e + slope
            across(am_f, 0, m, 16, OWN - 4)[...] = e - slope

        place = lax.rem(lane // 2, 6)
        halo = jnp.where(place == 0, pltpu.roll(land[phase, 2, 8:16, :], 120, 1), land[phase, BESIDE, 8:16, :])
        halo = jnp.where(place == 5, pltpu.roll(land[phase, 3, 8:16, :], 8, 1), halo)
        packed[8:16, :] = halo
        packed[7:8, :] = jnp.where(first, entry_packed[0:1, :], land[phase, 0, 15:16, :])
        packed[16:17, :] = jnp.where(last, packed[15:16, :], land[phase, 1, 8:9, :])
        beyond, mine = pltpu.roll(halo, inward, 1), pltpu.roll(pack[phase, 8:16, :], inward, 1)
        hs, _ = limit_all(
            halo, pltpu.roll(halo, 126, 1), pltpu.roll(halo, 2, 1), packed[9:17, :], packed[7:15, :], beyond, mine
        )
        near_face = halo - hs[2]

        right = [pltpu.roll(near_face, (121 - slot(m, 0)) % 128, 1) for m in range(6)]
        right[3] = right[3] * facing
        middle = roe(left, right, 2)
        middle[3] = middle[3] * facing

        ends = roe(
            [jnp.where(low_rows, across(ap_f, 0, m, 7)[...], across(ap_f, 0, m, 15, OWN - 4)[...]) for m in range(6)],
            [jnp.where(low_rows, across(am_f, 0, m, 8)[...], across(am_f, 0, m, 16, OWN - 4)[...]) for m in range(6)],
            1)
        for m in range(6):
            across(fa_f, 0, m, 8, OWN, 4)[...] = ends[m][0:4]
            across(fa_f, 0, m, 16, OWN - 4)[...] = ends[m]

        for c in range(4):
            u0, u1 = starts[c], []
            for m in range(6):
                inner = jnp.where(at_edge, pltpu.roll(middle[m], 6 - 2 * c, 1) if c < 3 else middle[m], inners[c][m])
                total = before[c][m] + inner + (fa[m, OWN + c, 9:17, :] - fa[m, OWN + c, 8:16, :])
                change = (-0.5 * STEP_SIZE) * total
                if m == 5:
                    change = change + STEP_SIZE * src[c]
                u1.append(u0[m] + change)
                out[m, c] = jnp.where(phase == 0, u0[m], out[m, c]) + 0.5 * change
            w = primitive(u1)
            for m in range(6):
                g[phase + 1, m, OWN + c, 8:16, :] = w[m]
        return carry

    load.wait()
    fill(0)
    pl.semaphore_wait(barrier, FAR + BESIDE + 1 - 4 * first.astype(jnp.int32) - 4 * last.astype(jnp.int32))
    lax.fori_loop(0, 2, section, 0)
    for phase in range(2):
        own_column(phase).wait_send()
        for along_axis in (True, False):
            each(MESSAGES, lambda k: far(phase, k).wait_send(), False, along_axis)
            each(PACKED, lambda k: direct(phase, k).wait_send(), False, along_axis)


def solution(mesh):
    def vmem(*shape):
        return pltpu.VMEM(shape, jnp.float32)

    def body(flow, inflow, wall_kind):
        padded = (6, PLANES, ROWS, 128)
        tiles = (6, 6, 8, 128)
        inner = (6, 4, 8, 128)
        copies = FAR + BESIDE + 1
        return pl.pallas_call(
            kernel,
            out_shape=pltpu.VMEM(flow.shape, jnp.float32),
            in_specs=[pl.BlockSpec(memory_space=pl.ANY)] * 3,
            out_specs=pl.BlockSpec(memory_space=pltpu.VMEM),
            scratch_shapes=[
                vmem(3, *padded), vmem(2, 24, 128), vmem(2, BESIDE + 1, 24, 128),
                vmem(24, 128), vmem(*tiles), vmem(*tiles), vmem(*tiles), vmem(*tiles), vmem(*tiles), vmem(*padded), vmem(*padded), vmem(*inner), vmem(*inner),
                vmem(4, 8, 128), vmem(*padded), vmem(ROWS, 128), vmem(2, 6, inflow.shape[1], 128), vmem(8, 128),
                pltpu.SMEM((2, wall_kind.shape[0]), jnp.int32),
                pltpu.SemaphoreType.DMA((4,)),
                pltpu.SemaphoreType.DMA((2, copies)), pltpu.SemaphoreType.DMA((2, copies)),
            ],
            compiler_params=pltpu.CompilerParams(
                collective_id=0, has_side_effects=True, vmem_limit_bytes=56 * 2**20
            ),
        )(flow, inflow, wall_kind.T)

    spec = P(None, "circ", "axial", "rad")
    return jax.shard_map(body, mesh=mesh, in_specs=(spec, P(), P()), out_specs=spec, check_vma=False)
```

```python
import jax
import jax.numpy as jnp
from jax import lax
from jax.experimental import pallas as pl
from jax.experimental.pallas import tpu as pltpu
from jax.sharding import PartitionSpec as P

MESH = pl.DeviceIdType.MESH
STEP_SIZE = 0.15
LIMIT_EPS = 0.03
FIX_WIDTH = 0.2
PRODUCE = 0.1355
DESTROY = 3.24

PLANES = 14
OWN = 5
ROWS = 24

MESSAGES = (
    (0, 1, (5, 9), (14, 16), (5, 9), (6, 8)),
    (0, -1, (5, 9), (8, 10), (5, 9), (16, 18)),
    (1, 1, (8, 9), (15, 16), (4, 5), (7, 8)),
    (1, -1, (8, 9), (8, 9), (4, 5), (16, 17)),
    (-1, 1, (5, 6), (15, 16), (9, 10), (7, 8)),
    (-1, -1, (5, 6), (8, 9), (9, 10), (16, 17)),
    (1, 0, (7, 9), (8, 16), (3, 5), (8, 16)),
    (-1, 0, (5, 7), (8, 16), (9, 11), (8, 16)),
)
PACKED = (
    (0, 1, (15, 20)),
    (0, -1, (4, 9)),
    (1, 0, (8, 16)),
    (-1, 0, (8, 16)),
)
FAR, BESIDE = len(MESSAGES), len(PACKED)


def slot(m, c):
    return 2 * (m * 6 + 1 + c)


def across(ref, phase, m, row, first=OWN, count=8):
    return ref.at[pl.ds(((phase * 6 + m) * PLANES + first) * ROWS + row, count, stride=ROWS), :]


def flat(ref):
    return ref.reshape(ref.size // 128, 128)


def conserved(p):
    q = 0.5 * (p[1] * p[1] + p[2] * p[2] + p[3] * p[3])
    return [p[0], p[0] * p[1], p[0] * p[2], p[0] * p[3], 2.5 * p[4] + p[0] * q, p[0] * p[5]]


def primitive(u):
    inv = 1.0 / u[0]
    v = [u[1] * inv, u[2] * inv, u[3] * inv]
    pressure = 0.4 * (u[4] - 0.5 * u[0] * (v[0] * v[0] + v[1] * v[1] + v[2] * v[2]))
    return [u[0], v[0], v[1], v[2], pressure, u[5] * inv]


def reach(*tiles):
    top = low = tiles[0]
    for t in tiles[1:]:
        top, low = jnp.maximum(top, t), jnp.minimum(low, t)
    return top, low


def limit(e, top, low, dc, ap, am, dr):
    da = ap - am
    top, low = jnp.maximum(top, jnp.maximum(ap, am)), jnp.minimum(low, jnp.minimum(ap, am))
    bound = jnp.minimum(top - e, e - low)
    delta = 0.25 * jnp.maximum(jnp.maximum(jnp.abs(dc), jnp.abs(da)), jnp.abs(dr))
    square = bound * bound + LIMIT_EPS
    cross = bound * delta
    factor = jnp.minimum(1.0, (square + 2.0 * cross) / (square + cross + 2.0 * delta * delta))
    quarter = 0.25 * factor
    return (quarter * dc, quarter * da, quarter * dr), (dc, da, dr)


def limit_all(e, cp, cm, ap, am, rp, rm):
    return limit(e, *reach(e, cp, cm, rp, rm), cp - cm, ap, am, rp - rm)


def fix(speed):
    size = jnp.abs(speed)
    return jnp.where(size < FIX_WIDTH, speed * speed * (0.5 / FIX_WIDTH) + 0.5 * FIX_WIDTH, size)


def side(s, d):
    y = lax.rsqrt(s[0])
    root = s[0] * y
    q = 0.5 * (s[1] * s[1] + s[2] * s[2] + s[3] * s[3])
    h = 3.5 * s[4] * (y * y) + q
    m = s[0] * s[d + 1]
    f = [m, m * s[1], m * s[2], m * s[3], m * h, m * s[5]]
    f[d + 1] = f[d + 1] + s[4]
    return root, h, f


def roe(left, right, d):
    rl, hl, fl = side(left, d)
    rr, hr, fr = side(right, d)
    jump = [r - l for l, r in zip(left, right)]
    w = rr / (rl + rr)
    vel = [left[k] + w * jump[k] for k in (1, 2, 3)]
    h = hl + w * (hr - hl)
    nu = left[5] + w * jump[5]
    un = vel[d]
    q = 0.5 * (vel[0] * vel[0] + vel[1] * vel[1] + vel[2] * vel[2])
    c2 = 0.4 * (h - q)
    ic = lax.rsqrt(c2)
    c = c2 * ic
    dens = rl * rr
    x = 0.5 * jump[4] * (ic * ic)
    y = 0.5 * dens * jump[d + 1] * ic
    mid = fix(un)
    slow = fix(un - c) * (x - y)
    fast = fix(un + c) * (x + y)
    both = slow + fast
    wave = mid * (jump[0] - 2.0 * x)
    total = both + wave
    skew = c * (fast - slow)
    shear = mid * dens
    dis = [total]
    inner = None
    for k in range(3):
        if k == d:
            dis.append(total * vel[k] + skew)
        else:
            part = shear * jump[k + 1]
            dis.append(total * vel[k] + part)
            inner = vel[k] * part if inner is None else inner + vel[k] * part
    dis.append(both * h + un * skew + wave * q + inner)
    dis.append(total * nu + shear * jump[5])
    return [fl[k] + fr[k] - dis[k] for k in range(6)]


def kernel(
    flow, inflow, walls, out,
    g, pack, land, packed, top, low, slant, lc, rc, ap, am, rin, rout, src, fa, ns, entry, entry_packed, kinds,
    local_sem, send_sem, recv_sem,
):
    ci, ai, ri = lax.axis_index("circ"), lax.axis_index("axial"), lax.axis_index("rad")
    nc, na = lax.axis_size("circ"), lax.axis_size("axial")
    first, last = ai == 0, ai == na - 1

    def target(dc, da, cross=False):
        return {"circ": lax.rem(ci + dc + nc, nc), "axial": ai + da, "rad": 1 - ri if cross else ri}

    twin = {"circ": ci, "axial": ai, "rad": 1 - ri}

    def guard(da, act):
        if da == 0:
            act()
        else:
            pl.when(ai < na - 1 if da > 0 else ai > 0)(act)

    barrier = pltpu.get_barrier_semaphore()
    for cross, group in ((False, MESSAGES), (True, PACKED)):
        for dc, da, *_ in group:
            guard(da, lambda dc=dc, da=da, cross=cross: pl.semaphore_signal(
                barrier, inc=1, device_id=target(dc, da, cross), device_id_type=MESH))
    pl.semaphore_signal(barrier, inc=1, device_id=twin, device_id_type=MESH)

    load = pltpu.make_async_copy(flow, g.at[0, :, OWN:OWN + 4, 8:16, :], local_sem.at[0])
    load.start()
    kind = pltpu.make_async_copy(walls, kinds, local_sem.at[1])
    kind.start()
    enter = [
        pltpu.make_async_copy(
            inflow.at[:, :, pl.ds(pl.multiple_of(core * 128, 128), 128)], entry.at[k], local_sem.at[2 + k])
        for k, core in enumerate((ri, 1 - ri))
    ]
    for part in enter:
        part.start()

    def remote(phase, k, source, into, device):
        return pltpu.make_async_remote_copy(
            src_ref=source, dst_ref=into, send_sem=send_sem.at[phase, k], recv_sem=recv_sem.at[phase, k],
            device_id=device, device_id_type=MESH,
        )

    def far(phase, k):
        dc, da, sp, sr, tp, tr = MESSAGES[k]
        return remote(
            phase, k, g.at[phase, :, sp[0]:sp[1], sr[0]:sr[1], :], g.at[phase, :, tp[0]:tp[1], tr[0]:tr[1], :],
            target(dc, da))

    def direct(phase, k):
        dc, da, (low, high) = PACKED[k]
        return remote(
            phase, FAR + k, pack.at[phase, low:high, :], land.at[phase, k, low:high, :], target(dc, da, True))

    def own_column(phase):
        return remote(phase, FAR + BESIDE, pack.at[phase, 8:16, :], land.at[phase, BESIDE, 8:16, :], twin)

    def each(group, act, back, kind):
        for k, (dc, da, *_) in enumerate(group):
            if kind in ("all", ("circ", "axial", "corner")[(da != 0) + (dc != 0 and da != 0)]):
                guard(-da if back else da, lambda k=k: act(k))

    lane = lax.broadcasted_iota(jnp.int32, (8, 128), 1)
    low_rows = lax.broadcasted_iota(jnp.int32, (8, 128), 0) < 4
    at_wall, at_edge = lane == 127 * ri, lane == 127 * (1 - ri)
    inward, outward = jnp.where(ri == 0, 127, 1), jnp.where(ri == 0, 1, 127)
    facing = jnp.where(ri == 0, 1.0, -1.0)
    radial = ri * 128 + lane
    wall_inv = 1.0 / (jnp.minimum(radial, 255 - radial) + 1).astype(jnp.float32)

    def around(e, near, sign):
        inner = pltpu.roll(jnp.where(at_wall, near, e), inward, 1)
        return inner, jnp.where(at_wall, e * sign, pltpu.roll(e, outward, 1))

    def signs(tile):
        return (1.0, tile, tile, -1.0, 1.0, tile)

    def fill(phase):
        tile = jnp.zeros((8, 128), jnp.float32)
        for m in range(6):
            for c in range(4):
                at = slot(m, c)
                e = g[phase, m, OWN + c, 8:16, :]
                turned = pltpu.roll(e, jnp.where(ri == 0, (at + 2) % 128, at), 1)
                tile = jnp.where((lane == at) | (lane == at + 1), turned, tile)
        pack[phase, 8:16, :] = tile
        for row, start in ((15, 16), (8, 4)):
            tile = jnp.zeros((4, 128), jnp.float32)
            for m in range(6):
                e = across(flat(g), phase, m, row, OWN, 4)[...]
                here = lane[0:4] == lax.rem(m + 127 * (1 - ri), 128)
                tile = jnp.where(here, pltpu.roll(e, m, 1) if m else e, tile)
            pack[phase, start:start + 4, :] = tile

    def station_signs():
        for row in range(7, 17):
            station = jnp.clip(ai * 8 + (row - 8), 0, na * 8 - 1)
            value = jnp.where(kinds[ri, station] == 1, -1.0, 1.0)
            ns[pl.ds(row, 1), :] = jnp.full((1, 128), value, jnp.float32)

    def entry_rows():
        row = jnp.zeros((1, 128), jnp.float32)
        for m in range(6):
            for c in range(-1, 5):
                at = lax.rem(ci * 4 + c + nc * 4, nc * 4)
                mine = entry[0, m, pl.ds(at, 1), :]
                for phase in range(2):
                    g[phase, m, OWN + c, 7:8, :] = mine
                if 0 <= c < 4:
                    theirs = entry[1, m, pl.ds(at, 1), :]
                    k = slot(m, c)
                    turned = pltpu.roll(
                        jnp.broadcast_to(theirs, (8, 128)), jnp.where(ri == 0, k, (k + 2) % 128), 1)[0:1]
                    row = jnp.where((lane[0:1] == k) | (lane[0:1] == k + 1), turned, row)
        entry_packed[0:1, :] = row

    def section(phase, carry):
        each(MESSAGES, lambda k: far(phase, k).start(), False, "axial")

        @pl.when(phase > 0)
        def _():
            fill(phase)

        each(PACKED, lambda k: direct(phase, k).start(), False, "axial")
        each(MESSAGES, lambda k: far(phase, k).start(), False, "corner")
        own_column(phase).start()
        each(PACKED, lambda k: direct(phase, k).start(), False, "circ")
        each(MESSAGES, lambda k: far(phase, k).start(), False, "circ")

        @pl.when(phase == 0)
        def _():
            kind.wait()
            for part in enter:
                part.wait()
            station_signs()
            pl.when(first)(entry_rows)

        def cell(m, c):
            return g[phase, m, OWN + c, 8:16, :]

        def turned(tile):
            return pltpu.roll(tile, jnp.where(ri == 0, 0, 126), 1)

        tile_sign = signs(ns[8:16, :])

        def prepare(c, columns, shift):
            for m in range(6):
                e = cell(m, c)
                inner, outer = around(e, pltpu.roll(columns, (128 - slot(m, shift)) % 128, 1), tile_sign[m])
                top[m, c + 1], low[m, c + 1] = reach(e, cell(m, c + 1), cell(m, c - 1), inner, outer)
                slant[m, c + 1] = inner - outer

        own_column(phase).wait_recv()
        each(MESSAGES, lambda k: far(phase, k).wait_recv(), True, "circ")
        ours = turned(land[phase, BESIDE, 8:16, :])
        for c in range(4):
            prepare(c, ours, c)

        each(MESSAGES, lambda k: far(phase, k).wait_recv(), True, "axial")

        @pl.when(last)
        def _():
            for m in range(6):
                for plane in range(OWN - 1, OWN + 5):
                    g[phase, m, plane, 16:17, :] = g[phase, m, plane, 15:16, :]

        def slopes(m, c):
            e = cell(m, c)
            return e, *limit(
                e, top[m, c + 1], low[m, c + 1], cell(m, c + 1) - cell(m, c - 1),
                g[phase, m, OWN + c, 9:17, :], g[phase, m, OWN + c, 7:15, :], slant[m, c + 1])

        def circ_face(c):
            return roe([lc[m, c] for m in range(6)], [rc[m, c + 1] for m in range(6)], 0)

        for c in range(4):
            diffs = []
            for m in range(6):
                e, hs, diff = slopes(m, c)
                diffs.append(diff)
                lc[m, c + 1] = e + hs[0]
                rc[m, c + 1] = e - hs[0]
                ap[m, OWN + c, 8:16, :] = e + hs[1]
                am[m, OWN + c, 8:16, :] = e - hs[1]
                scale = facing if m == 3 else 1.0
                rin[m, c] = (e + hs[2]) * scale
                rout[m, c] = (e - hs[2]) * scale
            oc = diffs[3][1] - diffs[2][2] * facing
            oa = diffs[1][2] * facing - diffs[3][0]
            orr = diffs[2][0] - diffs[1][1]
            s = jnp.sqrt(oc * oc + oa * oa + orr * orr)
            dens, nu = cell(0, c), cell(5, c)
            ratio = nu * wall_inv
            src[c] = (0.5 * PRODUCE) * s * dens * nu - DESTROY * dens * (ratio * ratio)

        radial_faces = []
        for c in range(4):
            ghost = [cell(m, c) * tile_sign[m] for m in range(6)]
            ghost[3] = ghost[3] * facing
            left = [jnp.where(at_wall, ghost[m], pltpu.roll(rin[m, c], outward, 1)) for m in range(6)]
            radial_faces.append(roe(left, [rout[m, c] for m in range(6)], 2))
        circ_faces = [None] + [circ_face(c) for c in range(1, 4)] + [None]


        each(PACKED, lambda k: direct(phase, k).wait_recv(), True, "circ")
        each(MESSAGES, lambda k: far(phase, k).wait_recv(), True, "corner")
        prepare(-1, turned(land[phase, 2, 8:16, :]), 3)
        prepare(4, turned(land[phase, 3, 8:16, :]), 0)

        for m in range(6):
            e, hs, _ = slopes(m, -1)
            lc[m, 0] = e + hs[0]
            e, hs, _ = slopes(m, 4)
            rc[m, 5] = e - hs[0]
        circ_faces[0], circ_faces[4] = circ_face(0), circ_face(4)

        for c in range(4):
            f = roe([ap[m, OWN + c, 7:15, :] for m in range(6)], [am[m, OWN + c, 8:16, :] for m in range(6)], 1)
            for m in range(6):
                fa[m, OWN + c, 8:16, :] = f[m]

        before, starts, inners = [], [], []
        for c in range(4):
            starts.append(conserved([cell(m, c) for m in range(6)]))
            before.append([])
            inners.append([])
            for m in range(6):
                face = radial_faces[c][m] * facing if m == 3 else radial_faces[c][m]
                inners[c].append(pltpu.roll(face, inward, 1))
                before[c].append((circ_faces[c + 1][m] - circ_faces[c][m]) - face)
        left = []
        for m in range(6):
            tile = rin[m, 0]
            for c in range(1, 4):
                tile = jnp.where(at_edge, rin[m, c], pltpu.roll(tile, 126, 1))
            left.append(tile)

        each(PACKED, lambda k: direct(phase, k).wait_recv(), True, "axial")

        g_f, ap_f, am_f, fa_f = flat(g), flat(ap), flat(am), flat(fa)

        def both(m, step_row, step_plane):
            return jnp.where(
                low_rows,
                across(g_f, phase, m, 7 + step_row, OWN + step_plane)[...],
                across(g_f, phase, m, 16 + step_row, OWN - 4 + step_plane)[...])

        row_sign = signs(jnp.where(
            low_rows, jnp.broadcast_to(ns[7:8, :], (8, 128)), jnp.broadcast_to(ns[16:17, :], (8, 128))))
        columns = jnp.where(low_rows, land[phase, 0, 16:24, :], land[phase, 1, 0:8, :])
        outside = (low_rows & first) | (jnp.logical_not(low_rows) & last)
        for m in range(6):
            e = both(m, 0, 0)
            inner, outer = around(e, pltpu.roll(columns, 128 - m, 1) if m else columns, row_sign[m])
            hs, _ = limit_all(e, both(m, 0, 1), both(m, 0, -1), both(m, 1, 0), both(m, -1, 0), inner, outer)
            slope = jnp.where(outside, 0.0, hs[1])
            across(ap_f, 0, m, 7, OWN)[...] = e + slope
            across(am_f, 0, m, 16, OWN - 4)[...] = e - slope

        place = lax.rem(lane // 2, 6)
        halo = jnp.where(place == 0, pltpu.roll(land[phase, 2, 8:16, :], 120, 1), land[phase, BESIDE, 8:16, :])
        halo = jnp.where(place == 5, pltpu.roll(land[phase, 3, 8:16, :], 8, 1), halo)
        packed[8:16, :] = halo
        packed[7:8, :] = jnp.where(first, entry_packed[0:1, :], land[phase, 0, 15:16, :])
        packed[16:17, :] = jnp.where(last, packed[15:16, :], land[phase, 1, 8:9, :])
        beyond, mine = pltpu.roll(halo, inward, 1), pltpu.roll(pack[phase, 8:16, :], inward, 1)
        hs, _ = limit_all(
            halo, pltpu.roll(halo, 126, 1), pltpu.roll(halo, 2, 1), packed[9:17, :], packed[7:15, :], beyond, mine
        )
        near_face = halo - hs[2]

        right = [pltpu.roll(near_face, (121 - slot(m, 0)) % 128, 1) for m in range(6)]
        right[3] = right[3] * facing
        middle = roe(left, right, 2)
        middle[3] = middle[3] * facing

        ends = roe(
            [jnp.where(low_rows, across(ap_f, 0, m, 7)[...], across(ap_f, 0, m, 15, OWN - 4)[...]) for m in range(6)],
            [jnp.where(low_rows, across(am_f, 0, m, 8)[...], across(am_f, 0, m, 16, OWN - 4)[...]) for m in range(6)],
            1)
        for m in range(6):
            across(fa_f, 0, m, 8, OWN, 4)[...] = ends[m][0:4]
            across(fa_f, 0, m, 16, OWN - 4)[...] = ends[m]

        for c in range(4):
            u0, u1 = starts[c], []
            for m in range(6):
                inner = jnp.where(at_edge, pltpu.roll(middle[m], 6 - 2 * c, 1) if c < 3 else middle[m], inners[c][m])
                total = before[c][m] + inner + (fa[m, OWN + c, 9:17, :] - fa[m, OWN + c, 8:16, :])
                change = (-0.5 * STEP_SIZE) * total
                if m == 5:
                    change = change + STEP_SIZE * src[c]
                u1.append(u0[m] + change)
                out[m, c] = jnp.where(phase == 0, u0[m], out[m, c]) + 0.5 * change
            w = primitive(u1)
            for m in range(6):
                g[phase + 1, m, OWN + c, 8:16, :] = w[m]
        return carry

    load.wait()
    fill(0)
    pl.semaphore_wait(barrier, FAR + BESIDE + 1 - 4 * first.astype(jnp.int32) - 4 * last.astype(jnp.int32))
    lax.fori_loop(0, 2, section, 0)
    for phase in range(2):
        own_column(phase).wait_send()
        each(MESSAGES, lambda k: far(phase, k).wait_send(), False, "all")
        each(PACKED, lambda k: direct(phase, k).wait_send(), False, "all")


def solution(mesh):
    def vmem(*shape):
        return pltpu.VMEM(shape, jnp.float32)

    def body(flow, inflow, wall_kind):
        padded = (6, PLANES, ROWS, 128)
        tiles = (6, 6, 8, 128)
        inner = (6, 4, 8, 128)
        copies = FAR + BESIDE + 1
        return pl.pallas_call(
            kernel,
            out_shape=pltpu.VMEM(flow.shape, jnp.float32),
            in_specs=[pl.BlockSpec(memory_space=pl.ANY)] * 3,
            out_specs=pl.BlockSpec(memory_space=pltpu.VMEM),
            scratch_shapes=[
                vmem(3, *padded), vmem(2, 24, 128), vmem(2, BESIDE + 1, 24, 128),
                vmem(24, 128), vmem(*tiles), vmem(*tiles), vmem(*tiles), vmem(*tiles), vmem(*tiles), vmem(*padded), vmem(*padded), vmem(*inner), vmem(*inner),
                vmem(4, 8, 128), vmem(*padded), vmem(ROWS, 128), vmem(2, 6, inflow.shape[1], 128), vmem(8, 128),
                pltpu.SMEM((2, wall_kind.shape[0]), jnp.int32),
                pltpu.SemaphoreType.DMA((4,)),
                pltpu.SemaphoreType.DMA((2, copies)), pltpu.SemaphoreType.DMA((2, copies)),
            ],
            compiler_params=pltpu.CompilerParams(
                collective_id=0, has_side_effects=True, vmem_limit_bytes=56 * 2**20
            ),
        )(flow, inflow, wall_kind.T)

    spec = P(None, "circ", "axial", "rad")
    return jax.shard_map(body, mesh=mesh, in_specs=(spec, P(), P()), out_specs=spec, check_vma=False)
```

```python
import jax
import jax.numpy as jnp
from jax import lax
from jax.experimental import pallas as pl
from jax.experimental.pallas import tpu as pltpu
from jax.sharding import PartitionSpec as P

MESH = pl.DeviceIdType.MESH
STEP_SIZE = 0.15
LIMIT_EPS = 0.03
FIX_WIDTH = 0.2
PRODUCE = 0.1355
DESTROY = 3.24

PLANES = 14
OWN = 5
ROWS = 24

MESSAGES = (
    (0, 1, (5, 9), (14, 16), (5, 9), (6, 8)),
    (0, -1, (5, 9), (8, 10), (5, 9), (16, 18)),
    (1, 1, (8, 9), (15, 16), (4, 5), (7, 8)),
    (1, -1, (8, 9), (8, 9), (4, 5), (16, 17)),
    (-1, 1, (5, 6), (15, 16), (9, 10), (7, 8)),
    (-1, -1, (5, 6), (8, 9), (9, 10), (16, 17)),
    (1, 0, (7, 9), (8, 16), (3, 5), (8, 16)),
    (-1, 0, (5, 7), (8, 16), (9, 11), (8, 16)),
)
PACKED = (
    (0, 1, (15, 20)),
    (0, -1, (4, 9)),
    (1, 0, (8, 16)),
    (-1, 0, (8, 16)),
)
FAR, BESIDE = len(MESSAGES), len(PACKED)


def slot(m, c):
    return 2 * (m * 6 + 1 + c)


def across(ref, phase, m, row, first=OWN, count=8):
    return ref.at[pl.ds(((phase * 6 + m) * PLANES + first) * ROWS + row, count, stride=ROWS), :]


def flat(ref):
    return ref.reshape(ref.size // 128, 128)


def conserved(p):
    q = 0.5 * (p[1] * p[1] + p[2] * p[2] + p[3] * p[3])
    return [p[0], p[0] * p[1], p[0] * p[2], p[0] * p[3], 2.5 * p[4] + p[0] * q, p[0] * p[5]]


def primitive(u):
    inv = 1.0 / u[0]
    v = [u[1] * inv, u[2] * inv, u[3] * inv]
    pressure = 0.4 * (u[4] - 0.5 * u[0] * (v[0] * v[0] + v[1] * v[1] + v[2] * v[2]))
    return [u[0], v[0], v[1], v[2], pressure, u[5] * inv]


def reach(*tiles):
    top = low = tiles[0]
    for t in tiles[1:]:
        top, low = jnp.maximum(top, t), jnp.minimum(low, t)
    return top, low


def limit(e, top, low, dc, ap, am, dr):
    da = ap - am
    top, low = jnp.maximum(top, jnp.maximum(ap, am)), jnp.minimum(low, jnp.minimum(ap, am))
    bound = jnp.minimum(top - e, e - low)
    delta = 0.25 * jnp.maximum(jnp.maximum(jnp.abs(dc), jnp.abs(da)), jnp.abs(dr))
    square = bound * bound + LIMIT_EPS
    cross = bound * delta
    factor = jnp.minimum(1.0, (square + 2.0 * cross) / (square + cross + 2.0 * delta * delta))
    quarter = 0.25 * factor
    return (quarter * dc, quarter * da, quarter * dr), (dc, da, dr)


def limit_all(e, cp, cm, ap, am, rp, rm):
    return limit(e, *reach(e, cp, cm, rp, rm), cp - cm, ap, am, rp - rm)


def fix(speed):
    size = jnp.abs(speed)
    return jnp.where(size < FIX_WIDTH, speed * speed * (0.5 / FIX_WIDTH) + 0.5 * FIX_WIDTH, size)


def side(s, d):
    y = lax.rsqrt(s[0])
    root = s[0] * y
    q = 0.5 * (s[1] * s[1] + s[2] * s[2] + s[3] * s[3])
    h = 3.5 * s[4] * (y * y) + q
    m = s[0] * s[d + 1]
    f = [m, m * s[1], m * s[2], m * s[3], m * h, m * s[5]]
    f[d + 1] = f[d + 1] + s[4]
    return root, h, f


def roe(left, right, d):
    rl, hl, fl = side(left, d)
    rr, hr, fr = side(right, d)
    jump = [r - l for l, r in zip(left, right)]
    w = rr / (rl + rr)
    vel = [left[k] + w * jump[k] for k in (1, 2, 3)]
    h = hl + w * (hr - hl)
    nu = left[5] + w * jump[5]
    un = vel[d]
    q = 0.5 * (vel[0] * vel[0] + vel[1] * vel[1] + vel[2] * vel[2])
    c2 = 0.4 * (h - q)
    ic = lax.rsqrt(c2)
    c = c2 * ic
    dens = rl * rr
    x = 0.5 * jump[4] * (ic * ic)
    y = 0.5 * dens * jump[d + 1] * ic
    mid = fix(un)
    slow = fix(un - c) * (x - y)
    fast = fix(un + c) * (x + y)
    both = slow + fast
    wave = mid * (jump[0] - 2.0 * x)
    total = both + wave
    skew = c * (fast - slow)
    shear = mid * dens
    dis = [total]
    inner = None
    for k in range(3):
        if k == d:
            dis.append(total * vel[k] + skew)
        else:
            part = shear * jump[k + 1]
            dis.append(total * vel[k] + part)
            inner = vel[k] * part if inner is None else inner + vel[k] * part
    dis.append(both * h + un * skew + wave * q + inner)
    dis.append(total * nu + shear * jump[5])
    return [fl[k] + fr[k] - dis[k] for k in range(6)]


def kernel(
    flow, inflow, walls, out,
    g, pack, land, packed, top, low, slant, lc, rc, ap, am, rin, rout, src, fa, ns, entry, entry_packed, kinds,
    local_sem, send_sem, recv_sem,
):
    ci, ai, ri = lax.axis_index("circ"), lax.axis_index("axial"), lax.axis_index("rad")
    nc, na = lax.axis_size("circ"), lax.axis_size("axial")
    first, last = ai == 0, ai == na - 1

    def target(dc, da, cross=False):
        return {"circ": lax.rem(ci + dc + nc, nc), "axial": ai + da, "rad": 1 - ri if cross else ri}

    twin = {"circ": ci, "axial": ai, "rad": 1 - ri}

    def guard(da, act):
        if da == 0:
            act()
        else:
            pl.when(ai < na - 1 if da > 0 else ai > 0)(act)

    barrier = pltpu.get_barrier_semaphore()
    for cross, group in ((False, MESSAGES), (True, PACKED)):
        for dc, da, *_ in group:
            guard(da, lambda dc=dc, da=da, cross=cross: pl.semaphore_signal(
                barrier, inc=1, device_id=target(dc, da, cross), device_id_type=MESH))
    pl.semaphore_signal(barrier, inc=1, device_id=twin, device_id_type=MESH)

    load = pltpu.make_async_copy(flow, g.at[0, :, OWN:OWN + 4, 8:16, :], local_sem.at[0])
    load.start()
    kind = pltpu.make_async_copy(walls, kinds, local_sem.at[1])
    kind.start()
    enter = [
        pltpu.make_async_copy(
            inflow.at[:, :, pl.ds(pl.multiple_of(core * 128, 128), 128)], entry.at[k], local_sem.at[2 + k])
        for k, core in enumerate((ri, 1 - ri))
    ]
    for part in enter:
        part.start()

    def remote(phase, k, source, into, device):
        return pltpu.make_async_remote_copy(
            src_ref=source, dst_ref=into, send_sem=send_sem.at[phase, k], recv_sem=recv_sem.at[phase, k],
            device_id=device, device_id_type=MESH,
        )

    def far(phase, k):
        dc, da, sp, sr, tp, tr = MESSAGES[k]
        return remote(
            phase, k, g.at[phase, :, sp[0]:sp[1], sr[0]:sr[1], :], g.at[phase, :, tp[0]:tp[1], tr[0]:tr[1], :],
            target(dc, da))

    def direct(phase, k):
        dc, da, (low, high) = PACKED[k]
        return remote(
            phase, FAR + k, pack.at[phase, low:high, :], land.at[phase, k, low:high, :], target(dc, da, True))

    def own_column(phase):
        return remote(phase, FAR + BESIDE, pack.at[phase, 8:16, :], land.at[phase, BESIDE, 8:16, :], twin)

    def each(group, act, back, kind):
        for k, (dc, da, *_) in enumerate(group):
            if kind in ("all", ("circ", "axial", "corner")[(da != 0) + (dc != 0 and da != 0)]):
                guard(-da if back else da, lambda k=k: act(k))

    lane = lax.broadcasted_iota(jnp.int32, (8, 128), 1)
    low_rows = lax.broadcasted_iota(jnp.int32, (8, 128), 0) < 4
    at_wall, at_edge = lane == 127 * ri, lane == 127 * (1 - ri)
    inward, outward = jnp.where(ri == 0, 127, 1), jnp.where(ri == 0, 1, 127)
    facing = jnp.where(ri == 0, 1.0, -1.0)
    radial = ri * 128 + lane
    wall_inv = 1.0 / (jnp.minimum(radial, 255 - radial) + 1).astype(jnp.float32)

    def around(e, near, sign):
        inner = pltpu.roll(jnp.where(at_wall, near, e), inward, 1)
        return inner, jnp.where(at_wall, e * sign, pltpu.roll(e, outward, 1))

    def signs(tile):
        return (1.0, tile, tile, -1.0, 1.0, tile)

    def fill(phase):
        tile = jnp.zeros((8, 128), jnp.float32)
        for m in range(6):
            for c in range(4):
                at = slot(m, c)
                e = g[phase, m, OWN + c, 8:16, :]
                turned = pltpu.roll(e, jnp.where(ri == 0, (at + 2) % 128, at), 1)
                tile = jnp.where((lane == at) | (lane == at + 1), turned, tile)
        pack[phase, 8:16, :] = tile
        for row, start in ((15, 16), (8, 4)):
            tile = jnp.zeros((4, 128), jnp.float32)
            for m in range(6):
                e = across(flat(g), phase, m, row, OWN, 4)[...]
                here = lane[0:4] == lax.rem(m + 127 * (1 - ri), 128)
                tile = jnp.where(here, pltpu.roll(e, m, 1) if m else e, tile)
            pack[phase, start:start + 4, :] = tile

    def station_signs():
        for row in range(7, 17):
            station = jnp.clip(ai * 8 + (row - 8), 0, na * 8 - 1)
            value = jnp.where(kinds[ri, station] == 1, -1.0, 1.0)
            ns[pl.ds(row, 1), :] = jnp.full((1, 128), value, jnp.float32)

    def entry_rows():
        row = jnp.zeros((1, 128), jnp.float32)
        for m in range(6):
            for c in range(-1, 5):
                at = lax.rem(ci * 4 + c + nc * 4, nc * 4)
                mine = entry[0, m, pl.ds(at, 1), :]
                for phase in range(2):
                    g[phase, m, OWN + c, 7:8, :] = mine
                if 0 <= c < 4:
                    theirs = entry[1, m, pl.ds(at, 1), :]
                    k = slot(m, c)
                    turned = pltpu.roll(
                        jnp.broadcast_to(theirs, (8, 128)), jnp.where(ri == 0, k, (k + 2) % 128), 1)[0:1]
                    row = jnp.where((lane[0:1] == k) | (lane[0:1] == k + 1), turned, row)
        entry_packed[0:1, :] = row

    def section(phase, carry):
        each(MESSAGES, lambda k: far(phase, k).start(), False, "axial")

        @pl.when(phase > 0)
        def _():
            fill(phase)

        each(PACKED, lambda k: direct(phase, k).start(), False, "axial")
        each(MESSAGES, lambda k: far(phase, k).start(), False, "corner")
        own_column(phase).start()
        each(PACKED, lambda k: direct(phase, k).start(), False, "circ")
        each(MESSAGES, lambda k: far(phase, k).start(), False, "circ")

        @pl.when(phase == 0)
        def _():
            kind.wait()
            for part in enter:
                part.wait()
            station_signs()
            pl.when(first)(entry_rows)

        def cell(m, c):
            return g[phase, m, OWN + c, 8:16, :]

        def turned(tile):
            return pltpu.roll(tile, jnp.where(ri == 0, 0, 126), 1)

        tile_sign = signs(ns[8:16, :])

        def prepare(c, columns, shift):
            for m in range(6):
                e = cell(m, c)
                inner, outer = around(e, pltpu.roll(columns, (128 - slot(m, shift)) % 128, 1), tile_sign[m])
                top[m, c + 1], low[m, c + 1] = reach(e, cell(m, c + 1), cell(m, c - 1), inner, outer)
                slant[m, c + 1] = inner - outer

        own_column(phase).wait_recv()
        each(MESSAGES, lambda k: far(phase, k).wait_recv(), True, "circ")
        ours = turned(land[phase, BESIDE, 8:16, :])
        for c in range(4):
            prepare(c, ours, c)

        each(MESSAGES, lambda k: far(phase, k).wait_recv(), True, "axial")

        @pl.when(last)
        def _():
            for m in range(6):
                for plane in range(OWN - 1, OWN + 5):
                    g[phase, m, plane, 16:17, :] = g[phase, m, plane, 15:16, :]

        def slopes(m, c):
            e = cell(m, c)
            return e, *limit(
                e, top[m, c + 1], low[m, c + 1], cell(m, c + 1) - cell(m, c - 1),
                g[phase, m, OWN + c, 9:17, :], g[phase, m, OWN + c, 7:15, :], slant[m, c + 1])

        def circ_face(c):
            return roe([lc[m, c] for m in range(6)], [rc[m, c + 1] for m in range(6)], 0)

        for c in range(4):
            diffs = []
            for m in range(6):
                e, hs, diff = slopes(m, c)
                diffs.append(diff)
                lc[m, c + 1] = e + hs[0]
                rc[m, c + 1] = e - hs[0]
                ap[m, OWN + c, 8:16, :] = e + hs[1]
                am[m, OWN + c, 8:16, :] = e - hs[1]
                scale = facing if m == 3 else 1.0
                rin[m, c] = (e + hs[2]) * scale
                rout[m, c] = (e - hs[2]) * scale
            oc = diffs[3][1] - diffs[2][2] * facing
            oa = diffs[1][2] * facing - diffs[3][0]
            orr = diffs[2][0] - diffs[1][1]
            s = jnp.sqrt(oc * oc + oa * oa + orr * orr)
            dens, nu = cell(0, c), cell(5, c)
            ratio = nu * wall_inv
            src[c] = (0.5 * PRODUCE) * s * dens * nu - DESTROY * dens * (ratio * ratio)

        radial_faces = []
        for c in range(4):
            ghost = [cell(m, c) * tile_sign[m] for m in range(6)]
            ghost[3] = ghost[3] * facing
            left = [jnp.where(at_wall, ghost[m], pltpu.roll(rin[m, c], outward, 1)) for m in range(6)]
            radial_faces.append(roe(left, [rout[m, c] for m in range(6)], 2))
        circ_faces = [None] + [circ_face(c) for c in range(1, 4)] + [None]


        each(PACKED, lambda k: direct(phase, k).wait_recv(), True, "circ")
        each(MESSAGES, lambda k: far(phase, k).wait_recv(), True, "corner")
        prepare(-1, turned(land[phase, 2, 8:16, :]), 3)
        prepare(4, turned(land[phase, 3, 8:16, :]), 0)

        for m in range(6):
            e, hs, _ = slopes(m, -1)
            lc[m, 0] = e + hs[0]
            e, hs, _ = slopes(m, 4)
            rc[m, 5] = e - hs[0]
        circ_faces[0], circ_faces[4] = circ_face(0), circ_face(4)

        for c in range(4):
            f = roe([ap[m, OWN + c, 7:15, :] for m in range(6)], [am[m, OWN + c, 8:16, :] for m in range(6)], 1)
            for m in range(6):
                fa[m, OWN + c, 8:16, :] = f[m]

        before, starts, inners = [], [], []
        for c in range(4):
            starts.append(conserved([cell(m, c) for m in range(6)]))
            before.append([])
            inners.append([])
            for m in range(6):
                face = radial_faces[c][m] * facing if m == 3 else radial_faces[c][m]
                inners[c].append(pltpu.roll(face, inward, 1))
                before[c].append((circ_faces[c + 1][m] - circ_faces[c][m]) - face)
        left = []
        for m in range(6):
            tile = rin[m, 0]
            for c in range(1, 4):
                tile = jnp.where(at_edge, rin[m, c], pltpu.roll(tile, 126, 1))
            left.append(tile)

        each(PACKED, lambda k: direct(phase, k).wait_recv(), True, "axial")

        g_f, ap_f, am_f, fa_f = flat(g), flat(ap), flat(am), flat(fa)

        def both(m, step_row, step_plane):
            return jnp.where(
                low_rows,
                across(g_f, phase, m, 7 + step_row, OWN + step_plane)[...],
                across(g_f, phase, m, 16 + step_row, OWN - 4 + step_plane)[...])

        row_sign = signs(jnp.where(
            low_rows, jnp.broadcast_to(ns[7:8, :], (8, 128)), jnp.broadcast_to(ns[16:17, :], (8, 128))))
        columns = jnp.where(low_rows, land[phase, 0, 16:24, :], land[phase, 1, 0:8, :])
        outside = (low_rows & first) | (jnp.logical_not(low_rows) & last)
        for m in range(6):
            e = both(m, 0, 0)
            inner, outer = around(e, pltpu.roll(columns, 128 - m, 1) if m else columns, row_sign[m])
            hs, _ = limit_all(e, both(m, 0, 1), both(m, 0, -1), both(m, 1, 0), both(m, -1, 0), inner, outer)
            slope = jnp.where(outside, 0.0, hs[1])
            across(ap_f, 0, m, 7, OWN)[...] = e + slope
            across(am_f, 0, m, 16, OWN - 4)[...] = e - slope

        place = lax.rem(lane // 2, 6)
        halo = jnp.where(place == 0, pltpu.roll(land[phase, 2, 8:16, :], 120, 1), land[phase, BESIDE, 8:16, :])
        halo = jnp.where(place == 5, pltpu.roll(land[phase, 3, 8:16, :], 8, 1), halo)
        packed[8:16, :] = halo
        packed[7:8, :] = jnp.where(first, entry_packed[0:1, :], land[phase, 0, 15:16, :])
        packed[16:17, :] = jnp.where(last, packed[15:16, :], land[phase, 1, 8:9, :])
        beyond, mine = pltpu.roll(halo, inward, 1), pltpu.roll(pack[phase, 8:16, :], inward, 1)
        hs, _ = limit_all(
            halo, pltpu.roll(halo, 126, 1), pltpu.roll(halo, 2, 1), packed[9:17, :], packed[7:15, :], beyond, mine
        )
        near_face = halo - hs[2]

        right = [pltpu.roll(near_face, (121 - slot(m, 0)) % 128, 1) for m in range(6)]
        right[3] = right[3] * facing
        middle = roe(left, right, 2)
        middle[3] = middle[3] * facing

        ends = roe(
            [jnp.where(low_rows, across(ap_f, 0, m, 7)[...], across(ap_f, 0, m, 15, OWN - 4)[...]) for m in range(6)],
            [jnp.where(low_rows, across(am_f, 0, m, 8)[...], across(am_f, 0, m, 16, OWN - 4)[...]) for m in range(6)],
            1)
        for m in range(6):
            across(fa_f, 0, m, 8, OWN, 4)[...] = ends[m][0:4]
            across(fa_f, 0, m, 16, OWN - 4)[...] = ends[m]

        for c in range(4):
            u0, u1 = starts[c], []
            for m in range(6):
                inner = jnp.where(at_edge, pltpu.roll(middle[m], 6 - 2 * c, 1) if c < 3 else middle[m], inners[c][m])
                total = before[c][m] + inner + (fa[m, OWN + c, 9:17, :] - fa[m, OWN + c, 8:16, :])
                change = (-0.5 * STEP_SIZE) * total
                if m == 5:
                    change = change + STEP_SIZE * src[c]
                u1.append(u0[m] + change)
                out[m, c] = (u0[m] if phase == 0 else out[m, c]) + 0.5 * change
            if phase == 0:
                w = primitive(u1)
                for m in range(6):
                    g[1, m, OWN + c, 8:16, :] = w[m]
        return carry

    load.wait()
    fill(0)
    pl.semaphore_wait(barrier, FAR + BESIDE + 1 - 4 * first.astype(jnp.int32) - 4 * last.astype(jnp.int32))
    for phase in range(2):
        section(phase, 0)
    for phase in range(2):
        own_column(phase).wait_send()
        each(MESSAGES, lambda k: far(phase, k).wait_send(), False, "all")
        each(PACKED, lambda k: direct(phase, k).wait_send(), False, "all")


def solution(mesh):
    def vmem(*shape):
        return pltpu.VMEM(shape, jnp.float32)

    def body(flow, inflow, wall_kind):
        padded = (6, PLANES, ROWS, 128)
        tiles = (6, 6, 8, 128)
        inner = (6, 4, 8, 128)
        copies = FAR + BESIDE + 1
        return pl.pallas_call(
            kernel,
            out_shape=pltpu.VMEM(flow.shape, jnp.float32),
            in_specs=[pl.BlockSpec(memory_space=pl.ANY)] * 3,
            out_specs=pl.BlockSpec(memory_space=pltpu.VMEM),
            scratch_shapes=[
                vmem(3, *padded), vmem(2, 24, 128), vmem(2, BESIDE + 1, 24, 128),
                vmem(24, 128), vmem(*tiles), vmem(*tiles), vmem(*tiles), vmem(*tiles), vmem(*tiles), vmem(*padded), vmem(*padded), vmem(*inner), vmem(*inner),
                vmem(4, 8, 128), vmem(*padded), vmem(ROWS, 128), vmem(2, 6, inflow.shape[1], 128), vmem(8, 128),
                pltpu.SMEM((2, wall_kind.shape[0]), jnp.int32),
                pltpu.SemaphoreType.DMA((4,)),
                pltpu.SemaphoreType.DMA((2, copies)), pltpu.SemaphoreType.DMA((2, copies)),
            ],
            compiler_params=pltpu.CompilerParams(
                collective_id=0, has_side_effects=True, vmem_limit_bytes=56 * 2**20
            ),
        )(flow, inflow, wall_kind.T)

    spec = P(None, "circ", "axial", "rad")
    return jax.shard_map(body, mesh=mesh, in_specs=(spec, P(), P()), out_specs=spec, check_vma=False)
```
